128 devices in a mesh: comp: 2 (over y_lo), gx: 8 (over x, y_hi), gy: 8 (over z, core).
Axes of the slice: x: 4, y: 4 (y_hi: 2, y_lo: 2; y = y_hi * 2 + y_lo), z: 4, core: 2. Of those that a mesh axis runs over, the one named last changes fastest.
Arguments:
- state: float32 [2, 30, 256, 2048], P('comp', None, 'gx', 'gy'), may hold values from -6 to 6
- conduct: float32 [2, 30, 256, 2048], P('comp', None, 'gx', 'gy'), may hold values from 0.3 to 3
- storage: float32 [2], P('comp'), may hold values from 0.05 to 0.5
- surface_source: float32 [2, 256, 2048], P('comp', 'gx', 'gy'), may hold values from -6 to 6
- plant_type: int32 [2, 256, 2048], P('comp', 'gx', 'gy'), may hold values from 0 to 15
- plant_table: float32 [16, 2], replicated, may hold values from 0.3 to 3
- layer_weights: float32 [2, 16, 6], replicated, may hold values from 0.05 to 1
- remap_rows: int32 [2, 256], P('comp', 'gx'), may hold values from 0 to 31
- remap_weights: float32 [2, 2048, 128], P('comp', 'gy'), may hold values from 0 to 1
Outputs:
- new_state: float32 [2, 30, 256, 2048], P('comp', None, 'gx', 'gy')
- exchange_flux: float32 [2, 256, 2048], P('comp', 'gx', 'gy')
The draws below stay inside these ranges and needn't reach their ends.
All inputs are finite; a program needn't handle non-finite values.
Results may differ from the reference program's by a relative error of at most 0.0003.
Values sent between devices are 32-bit elements; how exact they have to be, the bound alone decides.
A program may use at most 64 MiB of HBM per device.

```python
import math
import jax
import jax.numpy as jnp
from jax import lax

CX = 32
LV = 30
NS = 6
PATCH = 128
PLANTS = 16
ITERS = 3
NX = 256
NY = 2048


def draw_remap_weights(key, part):
    key_diag, key_off = jax.random.split(key)
    column = jnp.arange(NY) % PATCH
    eye = column[:, None] == jnp.arange(PATCH)[None, :]
    diag = jax.random.uniform(key_diag, (2, NY, 1), jnp.float32, 0.5, 1.0)
    off = jax.random.uniform(key_off, (2, NY, PATCH), jnp.float32, 0.0, 1.0) * (0.6 / PATCH)
    return jnp.where(eye[None], diag, off).astype(jnp.float32)


def place_ends(drawn, stream_key, least, top_value):
    index_at = [jax.random.randint(jax.random.fold_in(stream_key, axis), (), 0, length) for axis, length in enumerate(drawn.shape)]
    main_axis = drawn.shape.index(max(drawn.shape))
    next_to = index_at[:main_axis] + [(index_at[main_axis] + 1) % drawn.shape[main_axis]] + index_at[main_axis + 1:]
    return drawn.at[tuple(index_at)].set(least).at[tuple(next_to)].set(top_value)


def levels(key, dims, cuts, low, high):
    def one(axis_at, shards_of):
        heights = jax.random.uniform(jax.random.fold_in(jax.random.fold_in(key, 6), axis_at), (shards_of,), jnp.float32, low / len(cuts), high / len(cuts))
        return jnp.repeat(jnp.exp(heights), dims[axis_at] // shards_of).reshape((-1,) + (1,) * (len(dims) - axis_at - 1))

    gain = one(*cuts[0])
    for cut in cuts[1:]:
        gain = gain * one(*cut)
    return gain


def gaussian(stream_key, dims, width, bound, cuts=(), dtype=jnp.bfloat16):
    loudness = levels(stream_key, dims, cuts, -0.22, 0.18) if cuts else 1.0
    drawn = jax.random.normal(stream_key, dims, jnp.float32) * width * loudness
    return jnp.minimum(jnp.maximum(drawn, -bound), bound).astype(dtype)


def setup_inputs(seed: int = 0) -> dict:
    streams_of = jax.random.split(jax.random.key(seed), 10)
    state = gaussian(streams_of[0], (2, LV, NX, NY), 1.0, 6.0, ((0, 2), (2, 8), (3, 8)), jnp.float32)
    conduct = jnp.clip(jnp.exp(math.log(3.0) - 2.3025851 * jax.random.uniform(streams_of[1], (2, LV, NX, NY), jnp.float32) ** levels(streams_of[1], (2, LV, NX, NY), ((0, 2), (2, 8), (3, 8)), -0.2, 0.2)), 0.3, 3.0)
    storage = jnp.clip(jnp.exp(math.log(0.5) - 2.3025851 * jax.random.uniform(streams_of[2], (2,), jnp.float32) ** levels(streams_of[2], (2,), ((0, 2),), -0.2, 0.2)), 0.05, 0.5)
    surface_source = gaussian(streams_of[3], (2, NX, NY), 1.0, 6.0, ((0, 2), (1, 8), (2, 8)), jnp.float32)
    plant_type = place_ends(jax.random.randint(streams_of[4], (2, NX, NY), 0, PLANTS), jax.random.fold_in(streams_of[4], 1), 0, PLANTS - 1).astype(jnp.int32)
    plant_table = jnp.clip(jnp.exp(jax.random.uniform(streams_of[5], (PLANTS, 2), jnp.float32, math.log(0.3), math.log(3.0))), 0.3, 3.0)
    layer_weights = jnp.clip(jax.random.uniform(streams_of[6], (2, PLANTS, NS), jnp.float32, 0.05, 1.0), 0.05, 1.0)
    remap_rows = place_ends(jax.random.randint(streams_of[7], (2, NX), 0, CX), jax.random.fold_in(streams_of[7], 1), 0, CX - 1).astype(jnp.int32)
    remap_weights = draw_remap_weights(jax.random.fold_in(streams_of[9], 71), 0)
    return dict(state=state, conduct=conduct, storage=storage, surface_source=surface_source, plant_type=plant_type, plant_table=plant_table, layer_weights=layer_weights, remap_rows=remap_rows, remap_weights=remap_weights)


def apply_padded(vp, kp):
    v = vp[1:-1, 1:-1, 1:-1]
    kc = kp[1:-1, 1:-1, 1:-1]
    total = jnp.zeros_like(v)
    moves = [(2, 1, 1), (0, 1, 1), (1, 2, 1), (1, 0, 1), (1, 1, 2), (1, 1, 0)]
    for a, b, e in moves:
        vn = vp[a:a + v.shape[0], b:b + v.shape[1], e:e + v.shape[2]]
        kn = kp[a:a + v.shape[0], b:b + v.shape[1], e:e + v.shape[2]]
        total = total + 0.5 * (kc + kn) * (v - vn)
    return total

def least_squares(hmat, beta):
    gram = lax.optimization_barrier(jnp.sum(hmat[:, :, None] * hmat[:, None, :], axis=0))
    target_vector = beta * hmat[0, :]
    factor = jnp.linalg.cholesky(gram)
    return jax.scipy.linalg.cho_solve((factor, True), target_vector)

def reference(state, conduct, storage, surface_source, plant_type, plant_table, layer_weights, remap_rows, remap_weights):
    hp = lax.Precision.HIGHEST
    outs_state = []
    outs_flux = []
    for c in range(2):
        d = 1 - c
        rows = jnp.arange(NX) // CX * CX + remap_rows[c]
        src = state[d, :NS][:, rows, :]
        blocks = src.reshape(NS, NX, NY // PATCH, PATCH)
        wblk = remap_weights[c].reshape(NY // PATCH, PATCH, PATCH)
        remapped = jnp.einsum('lxbk,bjk->lxbj', blocks, wblk, precision=hp).reshape(NS, NX, NY)
        kinds = plant_type[c]
        own_prof = jnp.transpose(layer_weights[c][kinds], (2, 0, 1))
        other_prof = jnp.transpose(layer_weights[d][kinds], (2, 0, 1))
        own_force = lax.optimization_barrier(jnp.sum(own_prof * state[c, :NS], axis=0))
        other_force = lax.optimization_barrier(jnp.sum(other_prof * remapped, axis=0))
        if c == 0:
            atmospheric_forcing, soil_force = (own_force, other_force)
        else:
            atmospheric_forcing, soil_force = (other_force, own_force)
        params = plant_table[kinds]
        flux = params[:, :, 0] * (params[:, :, 1] * soil_force - atmospheric_forcing)
        sign = 1.0 - 2.0 * c
        top = sign * flux[None] * own_prof
        source = jnp.concatenate([top, jnp.zeros((LV - NS, NX, NY), jnp.float32)], axis=0)
        source = source.at[0].add(surface_source[c])
        field = state[c]
        keff = conduct[c] * (1.0 + 0.5 * jnp.tanh(field))
        kpad = jnp.pad(keff, 1)
        rhs = source - apply_padded(jnp.pad(field, 1), kpad)
        diagonal_shift = storage[c]
        beta = jnp.sqrt(jnp.sum(rhs * rhs))
        basis = [rhs / beta]
        hmat = jnp.zeros((ITERS + 1, ITERS), jnp.float32)
        for j in range(ITERS):
            krylov_vector = diagonal_shift * basis[j] + apply_padded(jnp.pad(basis[j], 1), kpad)
            for i in range(j + 1):
                h = jnp.sum(krylov_vector * basis[i])
                krylov_vector = krylov_vector - h * basis[i]
                hmat = hmat.at[i, j].set(h)
            nrm = jnp.sqrt(jnp.sum(krylov_vector * krylov_vector))
            hmat = hmat.at[j + 1, j].set(nrm)
            if j + 1 < ITERS:
                basis.append(krylov_vector / nrm)
        coef = least_squares(hmat, beta)
        update = field
        for j in range(ITERS):
            update = update + coef[j] * basis[j]
        outs_state.append(update)
        outs_flux.append(flux)
    return (jnp.stack(outs_state), jnp.stack(outs_flux))
```

```python
import jax
import jax.numpy as jnp
from jax import lax
from jax.experimental import pallas as pl
from jax.experimental.pallas import tpu as pltpu
from jax.sharding import PartitionSpec as P

MESH = pl.DeviceIdType.MESH
F32 = jnp.float32
NS = 6
PATCH = 128
PLANTS = 16
LV = 30
RX = 32
CY = 256
EX = 40
EY = 384
RIM = 3
EDGE = 96
SHIFT = 7.0
HP = lax.Precision.HIGHEST


def roll(x, shift, axis):
    return pltpu.roll(x, shift % x.shape[axis], axis)


def fold(x):
    total = None
    for r in range(0, RX, 8):
        for c in range(0, CY, 128):
            part = x[r : r + 8, c : c + 128]
            total = part if total is None else total + part
    return total


def far_first():
    offsets = []
    for dx in range(4):
        for dh in range(2):
            for dz in range(4):
                for co in range(2):
                    if (dx, dh, dz, co) != (0, 0, 0, 0):
                        hops = min(dx, 4 - dx) + 2 * dh + min(dz, 4 - dz)
                        offsets.append((hops, co, dx, dh, dz))
    return [(dx, dh, dz, co) for _, co, dx, dh, dz in sorted(offsets, reverse=True)]


def kernel(
    state,
    conduct,
    storage,
    surface,
    kinds_in,
    ptab,
    lw,
    rows,
    rw_in,
    out,
    flux_out,
    S,
    K,
    KX,
    KY,
    KZ,
    Q0,
    Q1,
    Q2,
    W0,
    W1,
    PART,
    SURF,
    KINDS,
    RW,
    TAB,
    OWN,
    MASK,
    PL1,
    PH1,
    RL1,
    RH1,
    PL2,
    PH2,
    RL2,
    RH2,
    ROW,
    GATH,
    lsem,
    ssem,
    rsem,
):
    c, gx, gy = lax.axis_index("comp"), lax.axis_index("gx"), lax.axis_index("gy")
    xp, xm = lax.rem(gx + 1, 8), lax.rem(gx + 7, 8)
    yp, ym = lax.rem(gy + 1, 8), lax.rem(gy + 7, 8)
    partner = (1 - c, gx, gy)

    local = [
        pltpu.make_async_copy(state.at[0], S.at[pl.ds(1, LV), pl.ds(0, RX), pl.ds(0, CY)], lsem.at[0]),
        pltpu.make_async_copy(conduct.at[0], K.at[pl.ds(1, LV), pl.ds(0, RX), pl.ds(0, CY)], lsem.at[1]),
        pltpu.make_async_copy(surface.at[0], SURF, lsem.at[2]),
        pltpu.make_async_copy(kinds_in.at[0], KINDS, lsem.at[3]),
        pltpu.make_async_copy(rw_in.at[0], RW, lsem.at[4]),
    ]
    for copy in local:
        copy.start()

    peers = [
        (
            c,
            lax.rem(gx // 2 + dx, 4) * 2 + lax.rem(gx + dh, 2),
            lax.rem(gy // 2 + dz, 4) * 2 + lax.rem(gy + co, 2),
        )
        for dx, dh, dz, co in far_first()
    ]
    barrier = pltpu.get_barrier_semaphore()
    for peer in peers + [partner]:
        pl.semaphore_signal(barrier, inc=1, device_id=peer, device_id_type=MESH)

    zero = jnp.zeros((EX, EY), F32)
    for ref in (S, K, Q0, Q1, Q2):
        ref[0] = zero
        ref[LV + 1] = zero
    row = lax.broadcasted_iota(jnp.int32, (EX, EY), 0)
    col = lax.broadcasted_iota(jnp.int32, (EX, EY), 1)
    row_ok = (
        (row < RX)
        | ((row < RX + RIM) & (gx < 7))
        | ((row >= EX - RIM) & (gx > 0))
    )
    col_ok = (
        (col < CY)
        | ((col < CY + RIM) & (gy < 7))
        | ((col >= EY - RIM) & (gy > 0))
    )
    MASK[...] = jnp.where(row_ok & col_ok, 1.0, 0.0).astype(F32)

    local[0].wait()
    local[1].wait()
    lane = lax.broadcasted_iota(jnp.int32, (RX, 128), 1)

    def edges(value, l, low, high):
        own = (lane >= RIM * l) & (lane < RIM * l + RIM)
        low = jnp.where(own, pltpu.roll(value[:, 0:128], RIM * l, 1), low)
        high = jnp.where(own, pltpu.roll(value[:, 128:256], RIM * l + RIM, 1), high)
        return low, high

    def make_keff(l, carry):
        low, high = carry
        s = S[l + 1, 0:RX, 0:CY]
        k = K[l + 1, 0:RX, 0:CY] * (1.0 + 0.5 * jnp.tanh(s))
        K[l + 1, 0:RX, 0:CY] = k
        low, high = edges(k, l, low, high)
        own = lane == EDGE + l
        low = jnp.where(own, pltpu.roll(s[:, 0:128], EDGE + l, 1), low)
        high = jnp.where(own, pltpu.roll(s[:, 128:256], EDGE + 1 + l, 1), high)
        return low, high

    blank = jnp.zeros((RX, 128), F32)
    low, high = lax.fori_loop(0, LV, make_keff, (blank, blank))
    PL1[...] = low
    PH1[...] = high

    pl.semaphore_wait(barrier, len(peers) + 1)

    sends = []

    def send(src, dst, device):
        i = len(sends)
        copy = pltpu.make_async_remote_copy(
            src_ref=src,
            dst_ref=dst,
            send_sem=ssem.at[i],
            recv_sem=rsem.at[i],
            device_id=device,
            device_id_type=MESH,
        )
        copy.start()
        sends.append(copy)
        return copy

    own_levels, own_columns = pl.ds(1, LV), pl.ds(0, CY)

    def send_rows(ref, width):
        return [
            send(
                ref.at[own_levels, pl.ds(0, width), own_columns],
                ref.at[own_levels, pl.ds(RX, width), own_columns],
                (c, xm, gy),
            ),
            send(
                ref.at[own_levels, pl.ds(RX - width, width), own_columns],
                ref.at[own_levels, pl.ds(EX - width, width), own_columns],
                (c, xp, gy),
            ),
        ]

    def send_packs(low_pack, high_pack, from_low, from_high):
        made = [
            send(low_pack, from_high.at[pl.ds(0, RX)], (c, gx, ym)),
            send(high_pack, from_low.at[pl.ds(0, RX)], (c, gx, yp)),
        ]
        for pack, landing, y in ((low_pack, from_high, ym), (high_pack, from_low, yp)):
            made.append(send(pack.at[pl.ds(0, RIM)], landing.at[pl.ds(RX, RIM)], (c, xm, y)))
            made.append(
                send(pack.at[pl.ds(RX - RIM, RIM)], landing.at[pl.ds(EX - RIM, RIM)], (c, xp, y))
            )
        return made

    levels_copy = send(state.at[0, pl.ds(0, NS)], PART, partner)
    first = send_rows(S, 1) + send_rows(K, RIM) + send_packs(PL1, PH1, RL1, RH1)

    local[2].wait()
    local[3].wait()
    local[4].wait()

    def look_up(r, carry):
        at = pl.ds(pl.multiple_of(r * 8, 8), 8)
        kinds = KINDS[at, :]
        found = [jnp.zeros((8, CY), F32) for _ in range(2 + 2 * NS)]
        for p in range(PLANTS):
            hit = kinds == p
            values = [ptab[p, 0], ptab[p, 1]]
            values += [lw[c, p, l] for l in range(NS)] + [lw[1 - c, p, l] for l in range(NS)]
            found = [jnp.where(hit, v, f) for v, f in zip(values, found)]
        for t, f in enumerate(found):
            TAB[t, at, :] = f
        own = jnp.zeros((8, CY), F32)
        for l in range(NS):
            own = own + found[2 + l] * S[l + 1, at, 0:CY]
        OWN[at, :] = own
        return carry

    lax.fori_loop(0, RX // 8, look_up, 0)
    pick_row = lax.broadcasted_iota(jnp.int32, (RX, RX), 0)
    pick_col = lax.broadcasted_iota(jnp.int32, (RX, RX), 1)
    wanted = jnp.zeros((RX, RX), jnp.int32)
    for x in range(RX):
        wanted = jnp.where(pick_row == x, rows[0, x], wanted)
    picker = jnp.where(wanted == pick_col, 1.0, 0.0).astype(F32)

    for copy in first:
        copy.wait_recv()

    mask = MASK[...]
    rim_lane = lax.broadcasted_iota(jnp.int32, (EX, 128), 1)

    def rim_tile(low_pack, high_pack, l):
        right = pltpu.roll(high_pack, lax.rem(128 - RIM * l, 128), 1)
        left = pltpu.roll(low_pack, lax.rem(253 - RIM * l, 128), 1)
        return jnp.where(rim_lane < RIM, right, jnp.where(rim_lane >= 128 - RIM, left, 0.0))

    def store_rim(ref, l, tile):
        ref[l, :, CY:EY] = jnp.where(mask[:, CY:EY] > 0.0, tile, 0.0)
        ref[l, RX:EX, 0:CY] = jnp.where(mask[RX:EX, 0:CY] > 0.0, ref[l, RX:EX, 0:CY], 0.0)

    def pairs(l, below):
        at = l - 1
        low_pack, high_pack = RL1[...], RH1[...]
        tile = rim_tile(low_pack, high_pack, at)
        k = jnp.concatenate([K[l, :, 0:CY], tile], axis=1)
        k = jnp.where(mask > 0.0, k, 0.0)
        KX[l] = 0.5 * (k + roll(k, -1, 0))
        KY[l] = 0.5 * (k + roll(k, -1, 1))
        KZ[l - 1] = 0.5 * (below + k)
        right = pltpu.roll(high_pack, 32 - at, 1)
        left = pltpu.roll(low_pack, 31 - at, 1)
        s_tile = jnp.where(rim_lane < 1, right, jnp.where(rim_lane >= 127, left, 0.0))
        store_rim(S, l, s_tile)
        return k

    top = lax.fori_loop(1, LV + 1, pairs, zero)
    KZ[LV] = 0.5 * top

    def flow(ref, l, v, down):
        fx = KX[l] * (v - roll(v, -1, 0))
        fy = KY[l] * (v - roll(v, -1, 1))
        up = KZ[l] * (v - ref[l + 1])
        return (fx - roll(fx, 1, 0)) + (fy - roll(fy, 1, 1)) + (up - down), up

    def residual(l, down):
        total, up = flow(S, l, S[l], down)
        Q0[l, 0:RX, 0:CY] = -total[0:RX, 0:CY]
        return up

    lax.fori_loop(1, LV + 1, residual, KZ[0] * (zero - S[1]))

    levels_copy.wait_recv()
    received = PART[...].reshape(NS * RX, CY)
    mixed = jnp.concatenate(
        [
            lax.dot_general(
                received[:, b : b + PATCH],
                RW[b : b + PATCH, :],
                (((1,), (1,)), ((), ())),
                precision=HP,
                preferred_element_type=F32,
            )
            for b in range(0, CY, PATCH)
        ],
        axis=1,
    )
    other = jnp.zeros((RX, CY), F32)
    for l in range(NS):
        remapped = jnp.dot(
            picker, mixed[l * RX : (l + 1) * RX], precision=HP, preferred_element_type=F32
        )
        other = other + TAB[2 + NS + l] * remapped
    own = OWN[...]
    is_air = c == 0
    air = jnp.where(is_air, own, other)
    soil = jnp.where(is_air, other, own)
    flux = TAB[0] * (TAB[1] * soil - air)
    flux_out[0] = flux
    signed = jnp.where(is_air, flux, -flux)
    for l in range(NS):
        value = Q0[l + 1, 0:RX, 0:CY] + signed * TAB[2 + l]
        if l == 0:
            value = value + SURF[...]
        Q0[l + 1, 0:RX, 0:CY] = value

    def pack_rhs(l, carry):
        return edges(Q0[l + 1, 0:RX, 0:CY], l, *carry)

    low, high = lax.fori_loop(0, LV, pack_rhs, (blank, blank))
    PL2[...] = low
    PH2[...] = high
    second = send_rows(Q0, RIM) + send_packs(PL2, PH2, RL2, RH2)
    for copy in second:
        copy.wait_recv()

    def unpack_rhs(l, carry):
        store_rim(Q0, l, rim_tile(RL2[...], RH2[...], l - 1))
        return carry

    lax.fori_loop(1, LV + 1, unpack_rhs, 0)

    shift = storage[0]
    scale = 1.0 / SHIFT

    def apply(q_ref, emit, sums):
        def level(l, carry):
            down, totals = carry
            v = q_ref[l]
            total, up = flow(q_ref, l, v, down)
            return up, emit(l, v, total, totals)

        first_down = KZ[0] * (zero - q_ref[1])
        none = tuple(jnp.zeros((8, 128), F32) for _ in range(sums))
        return lax.fori_loop(1, LV + 1, level, (first_down, none))[1]

    def emit0(l, v, total, sums):
        w = shift * v + total
        Q1[l] = (total * scale - v) * mask
        wi = w[0:RX, 0:CY]
        W0[l - 1] = wi
        return (sums[0] + fold(wi * v[0:RX, 0:CY]), sums[1] + fold(wi * wi))

    def emit1(l, v, total, sums):
        w = shift * v + total
        Q2[l] = (2.0 * (total * scale - v) - Q0[l]) * mask
        wi = w[0:RX, 0:CY]
        W1[l - 1] = wi
        return (
            sums[0] + fold(wi * Q0[l, 0:RX, 0:CY]),
            sums[1] + fold(wi * W0[l - 1]),
            sums[2] + fold(wi * wi),
        )

    def emit2(l, v, total, sums):
        wi = (shift * v + total)[0:RX, 0:CY]
        return (
            sums[0] + fold(wi * Q0[l, 0:RX, 0:CY]),
            sums[1] + fold(wi * W0[l - 1]),
            sums[2] + fold(wi * W1[l - 1]),
            sums[3] + fold(wi * wi),
        )

    b0, m00 = apply(Q0, emit0, 2)
    b1, m01, m11 = apply(Q1, emit1, 3)
    b2, m02, m12, m22 = apply(Q2, emit2, 4)
    one_lane = lax.broadcasted_iota(jnp.int32, (1, 128), 1)
    packed = jnp.zeros((1, 128), F32)
    for i, part in enumerate((b0, m00, b1, m01, m11, b2, m02, m12, m22)):
        packed = jnp.where(one_lane == i, jnp.sum(part, keepdims=True), packed)
    me = gx * 8 + gy
    ROW[0:1, :] = packed
    GATH[pl.ds(me, 1), :] = packed
    for peer in peers:
        pltpu.make_async_remote_copy(
            src_ref=ROW.at[pl.ds(0, 1)],
            dst_ref=GATH.at[pl.ds(me, 1)],
            send_sem=lsem.at[5],
            recv_sem=lsem.at[6],
            device_id=peer,
            device_id_type=MESH,
        ).start()
    all_rows = GATH.at[pl.ds(0, len(peers))]
    pltpu.make_async_copy(all_rows, all_rows, lsem.at[6]).wait()
    totals = jnp.sum(GATH[...], axis=0, keepdims=True)

    def at(i):
        return jnp.sum(jnp.where(one_lane == i, totals, 0.0), axis=1, keepdims=True)

    b0, m00, b1, m01, m11, b2, m02, m12, m22 = [at(i) for i in range(9)]
    l10, l20 = m01 / m00, m02 / m00
    d1 = m11 - m01 * l10
    e1 = m12 - m02 * l10
    l21 = e1 / d1
    d2 = m22 - m02 * l20 - e1 * l21
    z1 = b1 - l10 * b0
    z2 = b2 - l20 * b0 - l21 * z1
    y2 = z2 / d2
    y1 = z1 / d1 - l21 * y2
    y0 = b0 / m00 - l10 * y1 - l20 * y2

    def update(l, carry):
        out[0, l] = (
            S[l + 1, 0:RX, 0:CY]
            + y0 * Q0[l + 1, 0:RX, 0:CY]
            + y1 * Q1[l + 1, 0:RX, 0:CY]
            + y2 * Q2[l + 1, 0:RX, 0:CY]
        )
        return carry

    lax.fori_loop(0, LV, update, 0)
    pltpu.make_async_copy(all_rows, all_rows, lsem.at[5]).wait()
    for copy in sends:
        copy.wait_send()


def body(*args):
    any_spec = pl.BlockSpec(memory_space=pl.ANY)
    smem = pl.BlockSpec(memory_space=pltpu.SMEM)
    vmem = pl.BlockSpec(memory_space=pltpu.VMEM)
    field = pltpu.VMEM((LV + 2, EX, EY), F32)
    own = pltpu.VMEM((LV, RX, CY), F32)
    plane = pltpu.VMEM((RX, CY), F32)
    pack = pltpu.VMEM((RX, 128), F32)
    landing = pltpu.VMEM((EX, 128), F32)
    return pl.pallas_call(
        kernel,
        out_shape=(
            jax.ShapeDtypeStruct((1, LV, RX, CY), F32),
            jax.ShapeDtypeStruct((1, RX, CY), F32),
        ),
        in_specs=[any_spec, any_spec, smem, any_spec, any_spec, smem, smem, smem, any_spec],
        out_specs=(vmem, vmem),
        scratch_shapes=[
            field,
            field,
            field,
            field,
            field,
            field,
            field,
            field,
            own,
            own,
            pltpu.VMEM((NS, RX, CY), F32),
            plane,
            pltpu.VMEM((RX, CY), jnp.int32),
            pltpu.VMEM((CY, PATCH), F32),
            pltpu.VMEM((2 + 2 * NS, RX, CY), F32),
            plane,
            pltpu.VMEM((EX, EY), F32),
            pack,
            pack,
            landing,
            landing,
            pack,
            pack,
            landing,
            landing,
            pltpu.VMEM((8, 128), F32),
            pltpu.VMEM((64, 128), F32),
            pltpu.SemaphoreType.DMA((7,)),
            pltpu.SemaphoreType.DMA((24,)),
            pltpu.SemaphoreType.DMA((24,)),
        ],
        compiler_params=pltpu.CompilerParams(
            collective_id=0, has_side_effects=True, vmem_limit_bytes=40 * 1024 * 1024
        ),
    )(*args)


def solution(mesh):
    in_specs = (
        P("comp", None, "gx", "gy"),
        P("comp", None, "gx", "gy"),
        P("comp"),
        P("comp", "gx", "gy"),
        P("comp", "gx", "gy"),
        P(),
        P(),
        P("comp", "gx"),
        P("comp", "gy", None),
    )
    out_specs = (P("comp", None, "gx", "gy"), P("comp", "gx", "gy"))
    return jax.shard_map(body, mesh=mesh, in_specs=in_specs, out_specs=out_specs, check_vma=False)
```

```python
import jax
import jax.numpy as jnp
from jax import lax
from jax.experimental import pallas as pl
from jax.experimental.pallas import tpu as pltpu
from jax.sharding import PartitionSpec as P

MESH = pl.DeviceIdType.MESH
F32 = jnp.float32
NS = 6
PATCH = 128
PLANTS = 16
LV = 30
RX = 32
CY = 256
RIM = 3
TILES = 3
EX = 48
LOW, HIGH = 8, 40
OWN_ROWS = slice(LOW, HIGH)
EDGE = 96
SHIFT = 7.0
HP = lax.Precision.HIGHEST


def shifted(rows, by):
    return slice(rows.start + by, rows.stop + by)


def fold(x):
    return (x[0:8] + x[8:16]) + (x[16:24] + x[24:32])


def far_first():
    offsets = []
    for dx in range(4):
        for dh in range(2):
            for dz in range(4):
                for co in range(2):
                    if (dx, dh, dz, co) != (0, 0, 0, 0):
                        hops = min(dx, 4 - dx) + 2 * dh + min(dz, 4 - dz)
                        offsets.append((hops, co, dx, dh, dz))
    return [(dx, dh, dz, co) for _, co, dx, dh, dz in sorted(offsets, reverse=True)]


def kernel(
    state,
    conduct,
    storage,
    surface,
    kinds_in,
    ptab,
    lw,
    rows,
    rw_in,
    out,
    flux_out,
    S,
    K,
    KX,
    KY,
    KYM,
    KZ,
    Q0,
    Q1,
    Q2,
    W0,
    W1,
    PART,
    SURF,
    KINDS,
    RW,
    TAB,
    OWN,
    PL1,
    PH1,
    RL1,
    RH1,
    PL2,
    PH2,
    RL2,
    RH2,
    ROW,
    GATH,
    lsem,
    ssem,
    rsem,
):
    c, gx, gy = lax.axis_index("comp"), lax.axis_index("gx"), lax.axis_index("gy")
    xp, xm = lax.rem(gx + 1, 8), lax.rem(gx + 7, 8)
    yp, ym = lax.rem(gy + 1, 8), lax.rem(gy + 7, 8)
    partner = (1 - c, gx, gy)

    local = []
    for src, dst in ((state, S), (conduct, K)):
        for t in range(2):
            local.append(
                pltpu.make_async_copy(
                    src.at[0, :, :, pl.ds(128 * t, 128)],
                    dst.at[t, :, pl.ds(LOW, RX), :],
                    lsem.at[len(local)],
                )
            )
    for src, dst in ((surface, SURF), (kinds_in, KINDS), (rw_in, RW)):
        local.append(pltpu.make_async_copy(src.at[0], dst, lsem.at[len(local)]))
    for copy in local:
        copy.start()

    peers = [
        (
            c,
            lax.rem(gx // 2 + dx, 4) * 2 + lax.rem(gx + dh, 2),
            lax.rem(gy // 2 + dz, 4) * 2 + lax.rem(gy + co, 2),
        )
        for dx, dh, dz, co in far_first()
    ]
    barrier = pltpu.get_barrier_semaphore()
    for peer in peers + [partner]:
        pl.semaphore_signal(barrier, inc=1, device_id=peer, device_id_type=MESH)

    for copy in local[:4]:
        copy.wait()
    lane = lax.broadcasted_iota(jnp.int32, (RX, 128), 1)
    blank = jnp.zeros((RX, 128), F32)

    def edges(value0, value1, l, low, high):
        own = (lane >= RIM * l) & (lane < RIM * l + RIM)
        low = jnp.where(own, pltpu.roll(value0, RIM * l, 1), low)
        high = jnp.where(own, pltpu.roll(value1, RIM * l + RIM, 1), high)
        return low, high

    low, high = blank, blank
    for l in range(LV):
        s = [S[t, l, OWN_ROWS, :] for t in range(2)]
        k = [K[t, l, OWN_ROWS, :] * (1.0 + 0.5 * jnp.tanh(s[t])) for t in range(2)]
        for t in range(2):
            K[t, l, OWN_ROWS, :] = k[t]
        low, high = edges(k[0], k[1], l, low, high)
        own = lane == EDGE + l
        low = jnp.where(own, pltpu.roll(s[0], EDGE + l, 1), low)
        high = jnp.where(own, pltpu.roll(s[1], EDGE + 1 + l, 1), high)
    PL1[...] = low
    PH1[...] = high

    pl.semaphore_wait(barrier, len(peers) + 1)

    sends = []

    def send(src, dst, device):
        i = len(sends)
        copy = pltpu.make_async_remote_copy(
            src_ref=src,
            dst_ref=dst,
            send_sem=ssem.at[i],
            recv_sem=rsem.at[i],
            device_id=device,
            device_id_type=MESH,
        )
        copy.start()
        sends.append(copy)
        return copy

    own_tiles, own_levels = pl.ds(0, 2), pl.ds(0, LV)

    def send_rows(ref, width):
        return [
            send(
                ref.at[own_tiles, own_levels, pl.ds(LOW, width), :],
                ref.at[own_tiles, own_levels, pl.ds(HIGH, width), :],
                (c, xm, gy),
            ),
            send(
                ref.at[own_tiles, own_levels, pl.ds(HIGH - width, width), :],
                ref.at[own_tiles, own_levels, pl.ds(LOW - width, width), :],
                (c, xp, gy),
            ),
        ]

    def send_packs(low_pack, high_pack, from_low, from_high):
        made = [
            send(low_pack, from_high.at[pl.ds(LOW, RX)], (c, gx, ym)),
            send(high_pack, from_low.at[pl.ds(LOW, RX)], (c, gx, yp)),
        ]
        for pack, landing, y in ((low_pack, from_high, ym), (high_pack, from_low, yp)):
            made.append(send(pack.at[pl.ds(0, RIM)], landing.at[pl.ds(HIGH, RIM)], (c, xm, y)))
            made.append(
                send(pack.at[pl.ds(RX - RIM, RIM)], landing.at[pl.ds(LOW - RIM, RIM)], (c, xp, y))
            )
        return made

    levels_copy = send(state.at[0, pl.ds(0, NS)], PART, partner)
    first = send_rows(S, 1) + send_rows(K, RIM) + send_packs(PL1, PH1, RL1, RH1)

    for copy in local[4:]:
        copy.wait()

    def look_up(r, carry):
        at = pl.ds(pl.multiple_of(r * 8, 8), 8)
        below = pl.ds(pl.multiple_of(r * 8 + LOW, 8), 8)
        kinds = KINDS[at, :]
        found = [jnp.zeros((8, CY), F32) for _ in range(2 + 2 * NS)]
        for p in range(PLANTS):
            hit = kinds == p
            values = [ptab[0, p], ptab[1, p]]
            values += [lw[l, c, p] for l in range(NS)] + [lw[l, 1 - c, p] for l in range(NS)]
            found = [jnp.where(hit, v, f) for v, f in zip(values, found)]
        for t, f in enumerate(found):
            TAB[t, at, :] = f
        own = jnp.zeros((8, CY), F32)
        for l in range(NS):
            s = jnp.concatenate([S[0, l, below, :], S[1, l, below, :]], axis=1)
            own = own + found[2 + l] * s
        OWN[at, :] = own
        return carry

    lax.fori_loop(0, RX // 8, look_up, 0)
    pick_row = lax.broadcasted_iota(jnp.int32, (RX, RX), 0)
    pick_col = lax.broadcasted_iota(jnp.int32, (RX, RX), 1)
    wanted = jnp.zeros((RX, RX), jnp.int32)
    for x in range(RX):
        wanted = jnp.where(pick_row == x, rows[0, x], wanted)
    picker = jnp.where(wanted == pick_col, 1.0, 0.0).astype(F32)

    for copy in first:
        copy.wait_recv()

    row = lax.broadcasted_iota(jnp.int32, (EX, 128), 0)
    row_ok = (
        ((row >= LOW) & (row < HIGH))
        | ((row >= LOW - RIM) & (row < LOW) & (gx > 0))
        | ((row >= HIGH) & (row < HIGH + RIM) & (gx < 7))
    )

    def clean_packs(from_low, from_high):
        from_low[...] = jnp.where(row_ok & (gy > 0), from_low[...], 0.0)
        from_high[...] = jnp.where(row_ok & (gy < 7), from_high[...], 0.0)

    def clear_rows(ref, tiles, width):
        @pl.when(gx == 0)
        def _():
            for t in range(tiles):
                ref[t, :, LOW - width : LOW, :] = jnp.zeros((LV, width, 128), F32)

        @pl.when(gx == 7)
        def _():
            for t in range(tiles):
                ref[t, :, HIGH : HIGH + width, :] = jnp.zeros((LV, width, 128), F32)

    clean_packs(RL1, RH1)
    clear_rows(S, 2, 1)
    clear_rows(K, 2, RIM)

    def lanes_of(rows):
        return lax.broadcasted_iota(jnp.int32, (rows.stop - rows.start, 128), 1)

    def fill_rim(ref, from_low, from_high, rows):
        lane_at = lanes_of(rows)
        for l in range(LV):
            right = pltpu.roll(from_high[rows, :], (128 - RIM * l) % 128, 1)
            left = pltpu.roll(from_low[rows, :], (125 - RIM * l) % 128, 1)
            ref[2, l, rows, :] = jnp.where(
                lane_at < RIM, right, jnp.where(lane_at >= 128 - RIM, left, 0.0)
            )

    wide = slice(LOW - RIM, HIGH + RIM)
    fill_rim(K, RL1, RH1, wide)

    near = slice(LOW - 2, HIGH + 2)
    pair = slice(LOW - 3, HIGH + 2)
    lane_near = lanes_of(near)
    below = [None] * TILES
    for l in range(LV + 1):
        k = [K[t, l, near, :] for t in range(TILES)] if l < LV else None
        for t in range(TILES):
            if l == 0:
                KZ[t, l, near, :] = 0.5 * k[t]
            elif l == LV:
                KZ[t, l, near, :] = 0.5 * below[t]
            else:
                KZ[t, l, near, :] = 0.5 * (below[t] + k[t])
        if l == LV:
            break
        below = k
        high_side = [pltpu.roll(x, 127, 1) for x in k]
        low_side = [pltpu.roll(x, 1, 1) for x in k]
        for t in range(TILES):
            KX[t, l, pair, :] = 0.5 * (K[t, l, pair, :] + K[t, l, shifted(pair, 1), :])
            right = jnp.where(lane_near == 127, high_side[(t + 1) % 3], high_side[t])
            left = jnp.where(lane_near == 0, low_side[(t + 2) % 3], low_side[t])
            KY[t, l, near, :] = 0.5 * (k[t] + right)
            KYM[t, l, near, :] = 0.5 * (k[t] + left)

    def flow(ref, l, t, x, rows, right, left):
        total = KX[t, l, rows, :] * (x - ref[t, l, shifted(rows, 1), :])
        before = shifted(rows, -1)
        total = total + KX[t, l, before, :] * (x - ref[t, l, before, :])
        total = total + KY[t, l, rows, :] * (x - right)
        total = total + KYM[t, l, rows, :] * (x - left)
        up = x if l == LV - 1 else x - ref[t, l + 1, rows, :]
        down = x if l == 0 else x - ref[t, l - 1, rows, :]
        return total + (KZ[t, l + 1, rows, :] * up + KZ[t, l, rows, :] * down)

    first_lane, last_lane = lane == 0, lane == 127
    for l in range(LV):
        s = [S[t, l, OWN_ROWS, :] for t in range(2)]
        beyond = pltpu.roll(RH1[OWN_ROWS, :], 31 - l, 1)
        before = pltpu.roll(RL1[OWN_ROWS, :], 32 - l, 1)
        to_low = [pltpu.roll(x, 127, 1) for x in s] + [beyond]
        to_high = [pltpu.roll(x, 1, 1) for x in s] + [before]
        for t in range(2):
            right = jnp.where(last_lane, to_low[t + 1], to_low[t])
            left = jnp.where(first_lane, to_high[(t + 2) % 3], to_high[t])
            Q0[t, l, OWN_ROWS, :] = -flow(S, l, t, s[t], OWN_ROWS, right, left)

    levels_copy.wait_recv()
    received = PART[...].reshape(NS * RX, CY)
    mixed = jnp.concatenate(
        [
            lax.dot_general(
                received[:, b : b + PATCH],
                RW[b : b + PATCH, :],
                (((1,), (1,)), ((), ())),
                precision=HP,
                preferred_element_type=F32,
            )
            for b in range(0, CY, PATCH)
        ],
        axis=1,
    )
    other = jnp.zeros((RX, CY), F32)
    for l in range(NS):
        remapped = jnp.dot(
            picker, mixed[l * RX : (l + 1) * RX], precision=HP, preferred_element_type=F32
        )
        other = other + TAB[2 + NS + l] * remapped
    own = OWN[...]
    is_air = c == 0
    air = jnp.where(is_air, own, other)
    soil = jnp.where(is_air, other, own)
    flux = TAB[0] * (TAB[1] * soil - air)
    flux_out[0] = flux
    signed = jnp.where(is_air, flux, -flux)
    for l in range(NS):
        top = signed * TAB[2 + l]
        if l == 0:
            top = top + SURF[...]
        for t in range(2):
            Q0[t, l, OWN_ROWS, :] = Q0[t, l, OWN_ROWS, :] + top[:, 128 * t : 128 * t + 128]

    low, high = blank, blank
    for l in range(LV):
        low, high = edges(Q0[0, l, OWN_ROWS, :], Q0[1, l, OWN_ROWS, :], l, low, high)
    PL2[...] = low
    PH2[...] = high
    second = send_rows(Q0, RIM) + send_packs(PL2, PH2, RL2, RH2)
    for copy in second:
        copy.wait_recv()
    clean_packs(RL2, RH2)
    clear_rows(Q0, 2, RIM)
    fill_rim(Q0, RL2, RH2, wide)

    shift = storage[0]
    scale = 1.0 / SHIFT

    def apply(q_ref, rows, tiles, emit):
        lane_at = lanes_of(rows)
        for l in range(LV):
            x = [q_ref[t, l, rows, :] for t in range(TILES)]
            to_low = [pltpu.roll(v, 127, 1) for v in x]
            to_high = [pltpu.roll(v, 1, 1) for v in x]
            for t in range(tiles):
                right = jnp.where(lane_at == 127, to_low[(t + 1) % 3], to_low[t])
                left = jnp.where(lane_at == 0, to_high[(t + 2) % 3], to_high[t])
                emit(l, t, x[t], flow(q_ref, l, t, x[t], rows, right, left), rows)

    rim_ok = ((lane_near < RIM) & (gy < 7)) | ((lane_near >= 128 - RIM) & (gy > 0))
    rim_mask = jnp.where(rim_ok, 1.0, 0.0).astype(F32)

    def emit0(l, t, x, total, rows):
        q = total * scale - x
        if t < 2:
            W0[t, l, rows, :] = shift * x + total
        else:
            q = q * rim_mask
        Q1[t, l, rows, :] = q

    def emit1(l, t, x, total, rows):
        q = 2.0 * (total * scale - x) - Q0[t, l, rows, :]
        if t < 2:
            W1[t, l, rows, :] = shift * x + total
        else:
            q = q * rim_mask[0 : rows.stop - rows.start]
        Q2[t, l, rows, :] = q

    sums = [jnp.zeros((8, 128), F32) for _ in range(9)]

    def emit2(l, t, x, total, rows):
        w2 = shift * x + total
        w0, w1, q0 = W0[t, l, rows, :], W1[t, l, rows, :], Q0[t, l, rows, :]
        products = (w0 * q0, w0 * w0, w1 * q0, w1 * w0, w1 * w1, w2 * q0, w2 * w0, w2 * w1, w2 * w2)
        for i, product in enumerate(products):
            sums[i] = sums[i] + fold(product)

    apply(Q0, near, TILES, emit0)
    clear_rows(Q1, TILES, 2)
    apply(Q1, slice(LOW - 1, HIGH + 1), TILES, emit1)
    clear_rows(Q2, TILES, 1)
    apply(Q2, OWN_ROWS, 2, emit2)

    one_lane = lax.broadcasted_iota(jnp.int32, (1, 128), 1)
    packed = jnp.zeros((1, 128), F32)
    for i, part in enumerate(sums):
        packed = jnp.where(one_lane == i, jnp.sum(part, keepdims=True), packed)
    me = gx * 8 + gy
    ROW[0:1, :] = packed
    GATH[pl.ds(me, 1), :] = packed
    for peer in peers:
        pltpu.make_async_remote_copy(
            src_ref=ROW.at[pl.ds(0, 1)],
            dst_ref=GATH.at[pl.ds(me, 1)],
            send_sem=lsem.at[7],
            recv_sem=lsem.at[8],
            device_id=peer,
            device_id_type=MESH,
        ).start()
    all_rows = GATH.at[pl.ds(0, len(peers))]
    pltpu.make_async_copy(all_rows, all_rows, lsem.at[8]).wait()
    totals = jnp.sum(GATH[...], axis=0, keepdims=True)
    def at(i):
        return jnp.sum(jnp.where(one_lane == i, totals, 0.0), axis=1, keepdims=True)

    b0, m00, b1, m01, m11, b2, m02, m12, m22 = [at(i) for i in range(9)]
    l10, l20 = m01 / m00, m02 / m00
    d1 = m11 - m01 * l10
    e1 = m12 - m02 * l10
    l21 = e1 / d1
    d2 = m22 - m02 * l20 - e1 * l21
    z1 = b1 - l10 * b0
    z2 = b2 - l20 * b0 - l21 * z1
    y2 = z2 / d2
    y1 = z1 / d1 - l21 * y2
    y0 = b0 / m00 - l10 * y1 - l20 * y2

    for l in range(LV):
        for t in range(2):
            out[0, l, :, 128 * t : 128 * t + 128] = (
                S[t, l, OWN_ROWS, :]
                + y0 * Q0[t, l, OWN_ROWS, :]
                + y1 * Q1[t, l, OWN_ROWS, :]
                + y2 * Q2[t, l, OWN_ROWS, :]
            )
    pltpu.make_async_copy(all_rows, all_rows, lsem.at[7]).wait()
    for copy in sends:
        copy.wait_send()


def body(state, conduct, storage, surface, kinds, ptab, lw, rows, rw):
    hbm = pl.BlockSpec(memory_space=pltpu.HBM)
    smem = pl.BlockSpec(memory_space=pltpu.SMEM)
    vmem = pl.BlockSpec(memory_space=pltpu.VMEM)
    field = pltpu.VMEM((TILES, LV, EX, 128), F32)
    inner = pltpu.VMEM((2, LV, EX, 128), F32)
    plane = pltpu.VMEM((RX, CY), F32)
    pack = pltpu.VMEM((RX, 128), F32)
    landing = pltpu.VMEM((EX, 128), F32)
    return pl.pallas_call(
        kernel,
        out_shape=(
            jax.ShapeDtypeStruct((1, LV, RX, CY), F32),
            jax.ShapeDtypeStruct((1, RX, CY), F32),
        ),
        in_specs=[hbm, hbm, smem, hbm, hbm, smem, smem, smem, hbm],
        out_specs=(vmem, vmem),
        scratch_shapes=[
            inner,
            field,
            field,
            field,
            field,
            pltpu.VMEM((TILES, LV + 1, EX, 128), F32),
            field,
            field,
            field,
            inner,
            inner,
            pltpu.VMEM((NS, RX, CY), F32),
            plane,
            pltpu.VMEM((RX, CY), jnp.int32),
            pltpu.VMEM((CY, PATCH), F32),
            pltpu.VMEM((2 + 2 * NS, RX, CY), F32),
            plane,
            pack,
            pack,
            landing,
            landing,
            pack,
            pack,
            landing,
            landing,
            pltpu.VMEM((8, 128), F32),
            pltpu.VMEM((64, 128), F32),
            pltpu.SemaphoreType.DMA((9,)),
            pltpu.SemaphoreType.DMA((24,)),
            pltpu.SemaphoreType.DMA((24,)),
        ],
        compiler_params=pltpu.CompilerParams(
            collective_id=0, has_side_effects=True, vmem_limit_bytes=63 * 1024 * 1024
        ),
    )(state, conduct, storage, surface, kinds, ptab.T, jnp.transpose(lw, (2, 0, 1)), rows, rw)


def solution(mesh):
    in_specs = (
        P("comp", None, "gx", "gy"),
        P("comp", None, "gx", "gy"),
        P("comp"),
        P("comp", "gx", "gy"),
        P("comp", "gx", "gy"),
        P(),
        P(),
        P("comp", "gx"),
        P("comp", "gy", None),
    )
    out_specs = (P("comp", None, "gx", "gy"), P("comp", "gx", "gy"))
    return jax.shard_map(body, mesh=mesh, in_specs=in_specs, out_specs=out_specs, check_vma=False)
```

```python
import jax
import jax.numpy as jnp
from jax import lax
from jax.experimental import pallas as pl
from jax.experimental.pallas import tpu as pltpu
from jax.sharding import PartitionSpec as P

MESH = pl.DeviceIdType.MESH
F32 = jnp.float32
NS = 6
PATCH = 128
PLANTS = 16
LV = 30
RX = 32
CY = 256
RIM = 3
TILES = 3
EX = 48
LOW, HIGH = 8, 40
OWN_ROWS = slice(LOW, HIGH)
EDGE = 96
SHIFT = 7.0
HP = lax.Precision.HIGHEST


def shifted(rows, by):
    return slice(rows.start + by, rows.stop + by)


def fold(x):
    return (x[0:8] + x[8:16]) + (x[16:24] + x[24:32])


def far_first():
    offsets = []
    for dx in range(4):
        for dh in range(2):
            for dz in range(4):
                for co in range(2):
                    if (dx, dh, dz, co) != (0, 0, 0, 0):
                        hops = min(dx, 4 - dx) + 2 * dh + min(dz, 4 - dz)
                        offsets.append((hops, co, dx, dh, dz))
    return [(dx, dh, dz, co) for _, co, dx, dh, dz in sorted(offsets, reverse=True)]


def kernel(
    state,
    conduct,
    storage,
    surface,
    kinds_in,
    ptab,
    lw,
    rows,
    rw_in,
    out,
    flux_out,
    S,
    K,
    KX,
    KY,
    KYM,
    KZ,
    Q0,
    Q1,
    Q2,
    W0,
    W1,
    PART,
    SURF,
    KINDS,
    RW,
    TAB,
    OWN,
    PL1,
    PH1,
    RL1,
    RH1,
    PL2,
    PH2,
    RL2,
    RH2,
    PL3,
    PH3,
    RL3,
    RH3,
    ROW,
    GATH,
    lsem,
    ssem,
    rsem,
):
    c, gx, gy = lax.axis_index("comp"), lax.axis_index("gx"), lax.axis_index("gy")
    xp, xm = lax.rem(gx + 1, 8), lax.rem(gx + 7, 8)
    yp, ym = lax.rem(gy + 1, 8), lax.rem(gy + 7, 8)
    partner = (1 - c, gx, gy)

    local = []
    for src, dst in ((state, S), (conduct, K)):
        for t in range(2):
            local.append(
                pltpu.make_async_copy(
                    src.at[0, :, :, pl.ds(128 * t, 128)],
                    dst.at[t, :, pl.ds(LOW, RX), :],
                    lsem.at[len(local)],
                )
            )
    for src, dst in ((surface, SURF), (kinds_in, KINDS), (rw_in, RW)):
        local.append(pltpu.make_async_copy(src.at[0], dst, lsem.at[len(local)]))
    for copy in local:
        copy.start()

    peers = [
        (
            c,
            lax.rem(gx // 2 + dx, 4) * 2 + lax.rem(gx + dh, 2),
            lax.rem(gy // 2 + dz, 4) * 2 + lax.rem(gy + co, 2),
        )
        for dx, dh, dz, co in far_first()
    ]
    barrier = pltpu.get_barrier_semaphore()
    for peer in peers + [partner]:
        pl.semaphore_signal(barrier, inc=1, device_id=peer, device_id_type=MESH)

    for copy in local[:4]:
        copy.wait()
    lane = lax.broadcasted_iota(jnp.int32, (RX, 128), 1)
    blank = jnp.zeros((RX, 128), F32)

    def edges(value0, value1, l, low, high):
        own = (lane >= RIM * l) & (lane < RIM * l + RIM)
        low = jnp.where(own, pltpu.roll(value0, RIM * l, 1), low)
        high = jnp.where(own, pltpu.roll(value1, RIM * l + RIM, 1), high)
        return low, high

    low, high = blank, blank
    for l in range(LV):
        s = [S[t, l, OWN_ROWS, :] for t in range(2)]
        k = [K[t, l, OWN_ROWS, :] * (1.0 + 0.5 * jnp.tanh(s[t])) for t in range(2)]
        for t in range(2):
            K[t, l, OWN_ROWS, :] = k[t]
        low, high = edges(k[0], k[1], l, low, high)
        own = lane == EDGE + l
        low = jnp.where(own, pltpu.roll(s[0], EDGE + l, 1), low)
        high = jnp.where(own, pltpu.roll(s[1], EDGE + 1 + l, 1), high)
    PL1[...] = low
    PH1[...] = high

    pl.semaphore_wait(barrier, len(peers) + 1)

    sends = []

    def send(src, dst, device):
        i = len(sends)
        copy = pltpu.make_async_remote_copy(
            src_ref=src,
            dst_ref=dst,
            send_sem=ssem.at[i],
            recv_sem=rsem.at[i],
            device_id=device,
            device_id_type=MESH,
        )
        copy.start()
        sends.append(copy)
        return copy

    own_tiles = pl.ds(0, 2)

    def send_rows(ref, skip, width, levels):
        at, n = pl.ds(*levels), pl.ds
        return [
            send(
                ref.at[own_tiles, at, n(LOW + skip, width), :],
                ref.at[own_tiles, at, n(HIGH + skip, width), :],
                (c, xm, gy),
            ),
            send(
                ref.at[own_tiles, at, n(HIGH - skip - width, width), :],
                ref.at[own_tiles, at, n(LOW - skip - width, width), :],
                (c, xp, gy),
            ),
        ]

    def send_packs(low_pack, high_pack, from_low, from_high):
        return [
            send(low_pack, from_high.at[pl.ds(LOW, RX)], (c, gx, ym)),
            send(high_pack, from_low.at[pl.ds(LOW, RX)], (c, gx, yp)),
        ]

    def send_corners(low_pack, high_pack, from_low, from_high):
        made = []
        for pack, landing, y in ((low_pack, from_high, ym), (high_pack, from_low, yp)):
            made.append(send(pack.at[pl.ds(0, RIM)], landing.at[pl.ds(HIGH, RIM)], (c, xm, y)))
            made.append(
                send(pack.at[pl.ds(RX - RIM, RIM)], landing.at[pl.ds(LOW - RIM, RIM)], (c, xp, y))
            )
        return made

    every = (0, LV)
    first = send_rows(S, 0, 1, every) + send_rows(K, 0, 1, every) + send_packs(PL1, PH1, RL1, RH1)
    levels_copy = send(state.at[0, pl.ds(0, NS)], PART, partner)
    rest = send_corners(PL1, PH1, RL1, RH1) + send_rows(K, 1, RIM - 1, every)

    for copy in local[4:]:
        copy.wait()

    def look_up(r, carry):
        at = pl.ds(pl.multiple_of(r * 8, 8), 8)
        below = pl.ds(pl.multiple_of(r * 8 + LOW, 8), 8)
        kinds = KINDS[at, :]
        found = [jnp.zeros((8, CY), F32) for _ in range(2 + 2 * NS)]
        for p in range(PLANTS):
            hit = kinds == p
            values = [ptab[0, p], ptab[1, p]]
            values += [lw[l, c, p] for l in range(NS)] + [lw[l, 1 - c, p] for l in range(NS)]
            found = [jnp.where(hit, v, f) for v, f in zip(values, found)]
        for t, f in enumerate(found):
            TAB[t, at, :] = f
        own = jnp.zeros((8, CY), F32)
        for l in range(NS):
            s = jnp.concatenate([S[0, l, below, :], S[1, l, below, :]], axis=1)
            own = own + found[2 + l] * s
        OWN[at, :] = own
        return carry

    lax.fori_loop(0, RX // 8, look_up, 0)
    pick_row = lax.broadcasted_iota(jnp.int32, (RX, RX), 0)
    pick_col = lax.broadcasted_iota(jnp.int32, (RX, RX), 1)
    wanted = jnp.zeros((RX, RX), jnp.int32)
    for x in range(RX):
        wanted = jnp.where(pick_row == x, rows[0, x], wanted)
    picker = jnp.where(wanted == pick_col, 1.0, 0.0).astype(F32)

    for copy in first:
        copy.wait_recv()

    row = lax.broadcasted_iota(jnp.int32, (EX, 128), 0)
    row_ok = (
        ((row >= LOW) & (row < HIGH))
        | ((row >= LOW - RIM) & (row < LOW) & (gx > 0))
        | ((row >= HIGH) & (row < HIGH + RIM) & (gx < 7))
    )

    def clean_packs(from_low, from_high, spans):
        for span in spans:
            ok = row_ok[span]
            from_low[span, :] = jnp.where(ok & (gy > 0), from_low[span, :], 0.0)
            from_high[span, :] = jnp.where(ok & (gy < 7), from_high[span, :], 0.0)

    def clear_rows(ref, tiles, skip, width, levels):
        begin, count = levels
        blank_rows = jnp.zeros((count, width, 128), F32)

        @pl.when(gx == 0)
        def _():
            for t in range(tiles):
                ref[t, begin : begin + count, LOW - skip - width : LOW - skip, :] = blank_rows

        @pl.when(gx == 7)
        def _():
            for t in range(tiles):
                ref[t, begin : begin + count, HIGH + skip : HIGH + skip + width, :] = blank_rows

    clean_packs(RL1, RH1, (OWN_ROWS,))
    clear_rows(S, 2, 0, 1, every)
    clear_rows(K, 2, 0, 1, every)

    def lanes_of(rows):
        return lax.broadcasted_iota(jnp.int32, (rows.stop - rows.start, 128), 1)

    def fill_rim(ref, from_low, from_high, rows, levels):
        lane_at = lanes_of(rows)
        for l in range(levels[0], levels[0] + levels[1]):
            right = pltpu.roll(from_high[rows, :], (128 - RIM * l) % 128, 1)
            left = pltpu.roll(from_low[rows, :], (125 - RIM * l) % 128, 1)
            ref[2, l, rows, :] = jnp.where(
                lane_at < RIM, right, jnp.where(lane_at >= 128 - RIM, left, 0.0)
            )

    wide = slice(LOW - RIM, HIGH + RIM)
    near = slice(LOW - 2, HIGH + 2)
    lane_near = lanes_of(near)

    def vertical(t, l, rows):
        if l == 0:
            total = K[t, 0, rows, :]
        elif l == LV:
            total = K[t, LV - 1, rows, :]
        else:
            total = K[t, l - 1, rows, :] + K[t, l, rows, :]
        KZ[t, l, rows, :] = 0.5 * total

    def along_rows(t, l, rows):
        KX[t, l, rows, :] = 0.5 * (K[t, l, rows, :] + K[t, l, shifted(rows, 1), :])

    def flow(ref, l, t, x, rows, right, left):
        total = KX[t, l, rows, :] * (x - ref[t, l, shifted(rows, 1), :])
        before = shifted(rows, -1)
        total = total + KX[t, l, before, :] * (x - ref[t, l, before, :])
        total = total + KY[t, l, rows, :] * (x - right)
        total = total + KYM[t, l, rows, :] * (x - left)
        up = x if l == LV - 1 else x - ref[t, l + 1, rows, :]
        down = x if l == 0 else x - ref[t, l - 1, rows, :]
        return total + (KZ[t, l + 1, rows, :] * up + KZ[t, l, rows, :] * down)

    first_lane, last_lane = lane == 0, lane == 127

    def beside(values, beyond, before, t):
        to_low = [pltpu.roll(x, 127, 1) for x in values] + [beyond]
        to_high = [pltpu.roll(x, 1, 1) for x in values] + [before]
        right = jnp.where(last_lane, to_low[t + 1], to_low[t])
        left = jnp.where(first_lane, to_high[(t + 2) % 3], to_high[t])
        return right, left

    def residual(l, start):
        k = [K[t, l, OWN_ROWS, :] for t in range(2)]
        s = [S[t, l, OWN_ROWS, :] for t in range(2)]
        k_beyond = pltpu.roll(RH1[OWN_ROWS, :], (127 - RIM * l) % 128, 1)
        k_before = pltpu.roll(RL1[OWN_ROWS, :], (126 - RIM * l) % 128, 1)
        s_beyond = pltpu.roll(RH1[OWN_ROWS, :], 31 - l, 1)
        s_before = pltpu.roll(RL1[OWN_ROWS, :], 32 - l, 1)
        for t in range(2):
            if l == start:
                vertical(t, l, OWN_ROWS)
            if l + 1 != NS or start == NS:
                vertical(t, l + 1, OWN_ROWS)
            along_rows(t, l, slice(LOW - 1, HIGH))
            right, left = beside(k, k_beyond, k_before, t)
            KY[t, l, OWN_ROWS, :] = 0.5 * (k[t] + right)
            KYM[t, l, OWN_ROWS, :] = 0.5 * (k[t] + left)
            right, left = beside(s, s_beyond, s_before, t)
            Q0[t, l, OWN_ROWS, :] = -flow(S, l, t, s[t], OWN_ROWS, right, left)

    def send_basis(levels, pack_low, pack_high, from_low, from_high):
        low, high = blank, blank
        for l in range(levels[0], levels[0] + levels[1]):
            low, high = edges(Q0[0, l, OWN_ROWS, :], Q0[1, l, OWN_ROWS, :], l, low, high)
        pack_low[...] = low
        pack_high[...] = high
        packs = (pack_low, pack_high, from_low, from_high)
        return send_corners(*packs) + send_rows(Q0, 0, RIM, levels) + send_packs(*packs)

    for l in range(NS, LV):
        residual(l, NS)
    deep = (NS, LV - NS)
    deep_copies = send_basis(deep, PL2, PH2, RL2, RH2)
    for l in range(NS):
        residual(l, 0)

    levels_copy.wait_recv()
    received = PART[...].reshape(NS * RX, CY)
    mixed = jnp.concatenate(
        [
            lax.dot_general(
                received[:, b : b + PATCH],
                RW[b : b + PATCH, :],
                (((1,), (1,)), ((), ())),
                precision=HP,
                preferred_element_type=F32,
            )
            for b in range(0, CY, PATCH)
        ],
        axis=1,
    )
    other = jnp.zeros((RX, CY), F32)
    for l in range(NS):
        remapped = jnp.dot(
            picker, mixed[l * RX : (l + 1) * RX], precision=HP, preferred_element_type=F32
        )
        other = other + TAB[2 + NS + l] * remapped
    own = OWN[...]
    is_air = c == 0
    air = jnp.where(is_air, own, other)
    soil = jnp.where(is_air, other, own)
    flux = TAB[0] * (TAB[1] * soil - air)
    flux_out[0] = flux
    signed = jnp.where(is_air, flux, -flux)
    for l in range(NS):
        top = signed * TAB[2 + l]
        if l == 0:
            top = top + SURF[...]
        for t in range(2):
            Q0[t, l, OWN_ROWS, :] = Q0[t, l, OWN_ROWS, :] + top[:, 128 * t : 128 * t + 128]

    coupled = (0, NS)
    coupled_copies = send_basis(coupled, PL3, PH3, RL3, RH3)

    for copy in rest:
        copy.wait_recv()
    clean_packs(RL1, RH1, (slice(0, LOW), slice(HIGH, EX)))
    clear_rows(K, 2, 1, RIM - 1, every)
    fill_rim(K, RL1, RH1, wide, every)
    for l in range(LV + 1):
        for rows in (slice(LOW - 2, LOW), slice(HIGH, HIGH + 2)):
            for t in range(2):
                vertical(t, l, rows)
        vertical(2, l, near)
        if l == LV:
            break
        for t in range(2):
            along_rows(t, l, slice(LOW - 3, LOW - 1))
            along_rows(t, l, slice(HIGH, HIGH + 2))
        along_rows(2, l, slice(LOW - 3, HIGH + 2))
        for rows, tiles in ((slice(LOW - 2, LOW), (0, 1)), (slice(HIGH, HIGH + 2), (0, 1)), (near, (2,))):
            lane_at = lanes_of(rows)
            k = [K[t, l, rows, :] for t in range(TILES)]
            for t in tiles:
                beyond, before = pltpu.roll(k[(t + 1) % 3], 127, 1), pltpu.roll(k[(t + 2) % 3], 1, 1)
                right = jnp.where(lane_at == 127, beyond, pltpu.roll(k[t], 127, 1))
                left = jnp.where(lane_at == 0, before, pltpu.roll(k[t], 1, 1))
                KY[t, l, rows, :] = 0.5 * (k[t] + right)
                KYM[t, l, rows, :] = 0.5 * (k[t] + left)

    def land_basis(copies, levels, from_low, from_high):
        for copy in copies:
            copy.wait_recv()
        clean_packs(from_low, from_high, (slice(0, EX),))
        clear_rows(Q0, 2, 0, RIM, levels)
        fill_rim(Q0, from_low, from_high, wide, levels)

    shift = storage[0]
    scale = 1.0 / SHIFT

    def apply(q_ref, rows, tiles, emit, begin, end):
        lane_at = lanes_of(rows)
        for l in range(begin, end):
            x = [q_ref[t, l, rows, :] for t in range(TILES)]
            to_low = [pltpu.roll(v, 127, 1) for v in x]
            to_high = [pltpu.roll(v, 1, 1) for v in x]
            for t in range(tiles):
                right = jnp.where(lane_at == 127, to_low[(t + 1) % 3], to_low[t])
                left = jnp.where(lane_at == 0, to_high[(t + 2) % 3], to_high[t])
                emit(l, t, x[t], flow(q_ref, l, t, x[t], rows, right, left), rows)

    rim_ok = ((lane_near < RIM) & (gy < 7)) | ((lane_near >= 128 - RIM) & (gy > 0))
    rim_mask = jnp.where(rim_ok, 1.0, 0.0).astype(F32)

    def emit0(l, t, x, total, rows):
        q = total * scale - x
        if t < 2:
            W0[t, l, rows, :] = shift * x + total
        else:
            q = q * rim_mask
        Q1[t, l, rows, :] = q

    def emit1(l, t, x, total, rows):
        q = 2.0 * (total * scale - x) - Q0[t, l, rows, :]
        if t < 2:
            W1[t, l, rows, :] = shift * x + total
        else:
            q = q * rim_mask[0 : rows.stop - rows.start]
        Q2[t, l, rows, :] = q

    sums = [jnp.zeros((8, 128), F32) for _ in range(9)]

    def emit2(l, t, x, total, rows):
        w2 = shift * x + total
        w0, w1, q0 = W0[t, l, rows, :], W1[t, l, rows, :], Q0[t, l, rows, :]
        products = (w0 * q0, w0 * w0, w1 * q0, w1 * w0, w1 * w1, w2 * q0, w2 * w0, w2 * w1, w2 * w2)
        for i, product in enumerate(products):
            sums[i] = sums[i] + fold(product)

    def applications(begin, end):
        step = 1 if begin else 0
        apply(Q0, near, TILES, emit0, begin, end)
        clear_rows(Q1, TILES, 0, 2, (begin, end - begin))
        more = 0 if begin else 1
        begin, end = begin + step, end + more
        apply(Q1, slice(LOW - 1, HIGH + 1), TILES, emit1, begin, end)
        clear_rows(Q2, TILES, 0, 1, (begin, end - begin))
        begin, end = begin + step, end + more
        apply(Q2, OWN_ROWS, 2, emit2, begin, end)

    land_basis(deep_copies, deep, RL2, RH2)
    applications(NS + 1, LV)
    land_basis(coupled_copies, coupled, RL3, RH3)
    applications(0, NS + 1)

    one_lane = lax.broadcasted_iota(jnp.int32, (1, 128), 1)
    packed = jnp.zeros((1, 128), F32)
    for i, part in enumerate(sums):
        packed = jnp.where(one_lane == i, jnp.sum(part, keepdims=True), packed)
    me = gx * 8 + gy
    ROW[0:1, :] = packed
    GATH[pl.ds(me, 1), :] = packed
    for peer in peers:
        pltpu.make_async_remote_copy(
            src_ref=ROW.at[pl.ds(0, 1)],
            dst_ref=GATH.at[pl.ds(me, 1)],
            send_sem=lsem.at[7],
            recv_sem=lsem.at[8],
            device_id=peer,
            device_id_type=MESH,
        ).start()
    all_rows = GATH.at[pl.ds(0, len(peers))]
    pltpu.make_async_copy(all_rows, all_rows, lsem.at[8]).wait()
    totals = jnp.sum(GATH[...], axis=0, keepdims=True)
    def at(i):
        return jnp.sum(jnp.where(one_lane == i, totals, 0.0), axis=1, keepdims=True)

    b0, m00, b1, m01, m11, b2, m02, m12, m22 = [at(i) for i in range(9)]
    l10, l20 = m01 / m00, m02 / m00
    d1 = m11 - m01 * l10
    e1 = m12 - m02 * l10
    l21 = e1 / d1
    d2 = m22 - m02 * l20 - e1 * l21
    z1 = b1 - l10 * b0
    z2 = b2 - l20 * b0 - l21 * z1
    y2 = z2 / d2
    y1 = z1 / d1 - l21 * y2
    y0 = b0 / m00 - l10 * y1 - l20 * y2

    for l in range(LV):
        for t in range(2):
            out[0, l, :, 128 * t : 128 * t + 128] = (
                S[t, l, OWN_ROWS, :]
                + y0 * Q0[t, l, OWN_ROWS, :]
                + y1 * Q1[t, l, OWN_ROWS, :]
                + y2 * Q2[t, l, OWN_ROWS, :]
            )
    pltpu.make_async_copy(all_rows, all_rows, lsem.at[7]).wait()
    for copy in sends:
        copy.wait_send()


def body(state, conduct, storage, surface, kinds, ptab, lw, rows, rw):
    hbm = pl.BlockSpec(memory_space=pltpu.HBM)
    smem = pl.BlockSpec(memory_space=pltpu.SMEM)
    vmem = pl.BlockSpec(memory_space=pltpu.VMEM)
    field = pltpu.VMEM((TILES, LV, EX, 128), F32)
    inner = pltpu.VMEM((2, LV, EX, 128), F32)
    plane = pltpu.VMEM((RX, CY), F32)
    pack = pltpu.VMEM((RX, 128), F32)
    landing = pltpu.VMEM((EX, 128), F32)
    return pl.pallas_call(
        kernel,
        out_shape=(
            jax.ShapeDtypeStruct((1, LV, RX, CY), F32),
            jax.ShapeDtypeStruct((1, RX, CY), F32),
        ),
        in_specs=[hbm, hbm, smem, hbm, hbm, smem, smem, smem, hbm],
        out_specs=(vmem, vmem),
        scratch_shapes=[
            inner,
            field,
            field,
            field,
            field,
            pltpu.VMEM((TILES, LV + 1, EX, 128), F32),
            field,
            field,
            field,
            inner,
            inner,
            pltpu.VMEM((NS, RX, CY), F32),
            plane,
            pltpu.VMEM((RX, CY), jnp.int32),
            pltpu.VMEM((CY, PATCH), F32),
            pltpu.VMEM((2 + 2 * NS, RX, CY), F32),
            plane,
            pack,
            pack,
            landing,
            landing,
            pack,
            pack,
            landing,
            landing,
            pack,
            pack,
            landing,
            landing,
            pltpu.VMEM((8, 128), F32),
            pltpu.VMEM((64, 128), F32),
            pltpu.SemaphoreType.DMA((9,)),
            pltpu.SemaphoreType.DMA((32,)),
            pltpu.SemaphoreType.DMA((32,)),
        ],
        compiler_params=pltpu.CompilerParams(
            collective_id=0, has_side_effects=True, vmem_limit_bytes=66_000_000
        ),
    )(state, conduct, storage, surface, kinds, ptab.T, jnp.transpose(lw, (2, 0, 1)), rows, rw)


def solution(mesh):
    in_specs = (
        P("comp", None, "gx", "gy"),
        P("comp", None, "gx", "gy"),
        P("comp"),
        P("comp", "gx", "gy"),
        P("comp", "gx", "gy"),
        P(),
        P(),
        P("comp", "gx"),
        P("comp", "gy", None),
    )
    out_specs = (P("comp", None, "gx", "gy"), P("comp", "gx", "gy"))
    return jax.shard_map(body, mesh=mesh, in_specs=in_specs, out_specs=out_specs, check_vma=False)
```

```python
import jax
import jax.numpy as jnp
from jax import lax
from jax.experimental import pallas as pl
from jax.experimental.pallas import tpu as pltpu
from jax.sharding import PartitionSpec as P

MESH = pl.DeviceIdType.MESH
F32 = jnp.float32
NS = 6
PATCH = 128
PLANTS = 16
LV = 30
RX = 32
CY = 256
RIM = 3
TILES = 3
EX = 48
LOW, HIGH = 8, 40
OWN_ROWS = slice(LOW, HIGH)
EDGE = 96
SHIFT = 7.0
HP = lax.Precision.HIGHEST


def shifted(rows, by):
    return slice(rows.start + by, rows.stop + by)


def fold(x):
    return (x[0:8] + x[8:16]) + (x[16:24] + x[24:32])


def far_first():
    offsets = []
    for dx in range(4):
        for dh in range(2):
            for dz in range(4):
                for co in range(2):
                    if (dx, dh, dz, co) != (0, 0, 0, 0):
                        hops = min(dx, 4 - dx) + 2 * dh + min(dz, 4 - dz)
                        offsets.append((hops, co, dx, dh, dz))
    return [(dx, dh, dz, co) for _, co, dx, dh, dz in sorted(offsets, reverse=True)]


def kernel(
    state,
    conduct,
    storage,
    surface,
    kinds_in,
    ptab,
    lw,
    rows,
    rw_in,
    out,
    flux_out,
    S,
    K,
    KX,
    KY,
    KYM,
    KZ,
    Q0,
    Q1,
    Q2,
    W0,
    W1,
    PART,
    SURF,
    KINDS,
    RW,
    TAB,
    OWN,
    PL1,
    PH1,
    RL1,
    RH1,
    PL2,
    PH2,
    RL2,
    RH2,
    PL3,
    PH3,
    RL3,
    RH3,
    ROW,
    GATH,
    NEW,
    FLUX,
    lsem,
    ssem,
    rsem,
    near_sem,
    far_sem,
):
    c, gx, gy = lax.axis_index("comp"), lax.axis_index("gx"), lax.axis_index("gy")
    xp, xm = lax.rem(gx + 1, 8), lax.rem(gx + 7, 8)
    yp, ym = lax.rem(gy + 1, 8), lax.rem(gy + 7, 8)
    partner = (1 - c, gx, gy)

    local = []
    for src, dst in ((state, S), (conduct, K)):
        for t in range(2):
            local.append(
                pltpu.make_async_copy(
                    src.at[0, :, :, pl.ds(128 * t, 128)],
                    dst.at[t, :, pl.ds(LOW, RX), :],
                    lsem.at[len(local)],
                )
            )
    for src, dst in ((surface, SURF), (kinds_in, KINDS), (rw_in, RW)):
        local.append(pltpu.make_async_copy(src.at[0], dst, lsem.at[len(local)]))
    for copy in local:
        copy.start()

    peers = [
        (
            c,
            lax.rem(gx // 2 + dx, 4) * 2 + lax.rem(gx + dh, 2),
            lax.rem(gy // 2 + dz, 4) * 2 + lax.rem(gy + co, 2),
        )
        for dx, dh, dz, co in far_first()
    ]
    barrier = pltpu.get_barrier_semaphore()
    ring = [(i, j) for i in (0, 1, -1) for j in (0, 1, -1) if (i, j) != (0, 0)]

    def at_offset(i, j):
        return (c, lax.rem(gx + 8 + i, 8), lax.rem(gy + 8 + j, 8))

    neighbours = [at_offset(i, j) for i, j in ring]
    for peer in neighbours + [partner]:
        pl.semaphore_signal(barrier, inc=1, device_id=peer, device_id_type=MESH)

    for copy in local[:4]:
        copy.wait()
    lane = lax.broadcasted_iota(jnp.int32, (RX, 128), 1)
    blank = jnp.zeros((RX, 128), F32)

    def edges(value0, value1, l, low, high):
        own = (lane >= RIM * l) & (lane < RIM * l + RIM)
        low = jnp.where(own, pltpu.roll(value0, RIM * l, 1), low)
        high = jnp.where(own, pltpu.roll(value1, RIM * l + RIM, 1), high)
        return low, high

    low, high = blank, blank
    for l in range(LV):
        s = [S[t, l, OWN_ROWS, :] for t in range(2)]
        k = [K[t, l, OWN_ROWS, :] * (1.0 + 0.5 * jnp.tanh(s[t])) for t in range(2)]
        for t in range(2):
            K[t, l, OWN_ROWS, :] = k[t]
        low, high = edges(k[0], k[1], l, low, high)
        own = lane == EDGE + l
        low = jnp.where(own, pltpu.roll(s[0], EDGE + l, 1), low)
        high = jnp.where(own, pltpu.roll(s[1], EDGE + 1 + l, 1), high)
    PL1[...] = low
    PH1[...] = high

    pl.semaphore_wait(barrier, len(neighbours) + 1)

    sends = []

    def send(src, dst, device):
        i = len(sends)
        copy = pltpu.make_async_remote_copy(
            src_ref=src,
            dst_ref=dst,
            send_sem=ssem.at[i],
            recv_sem=rsem.at[i],
            device_id=device,
            device_id_type=MESH,
        )
        copy.start()
        sends.append(copy)
        return copy

    own_tiles = pl.ds(0, 2)

    def send_rows(ref, skip, width, levels):
        at, n = pl.ds(*levels), pl.ds
        return [
            send(
                ref.at[own_tiles, at, n(LOW + skip, width), :],
                ref.at[own_tiles, at, n(HIGH + skip, width), :],
                (c, xm, gy),
            ),
            send(
                ref.at[own_tiles, at, n(HIGH - skip - width, width), :],
                ref.at[own_tiles, at, n(LOW - skip - width, width), :],
                (c, xp, gy),
            ),
        ]

    def send_packs(low_pack, high_pack, from_low, from_high):
        return [
            send(low_pack, from_high.at[pl.ds(LOW, RX)], (c, gx, ym)),
            send(high_pack, from_low.at[pl.ds(LOW, RX)], (c, gx, yp)),
        ]

    def send_corners(low_pack, high_pack, from_low, from_high):
        made = []
        for pack, landing, y in ((low_pack, from_high, ym), (high_pack, from_low, yp)):
            made.append(send(pack.at[pl.ds(0, RIM)], landing.at[pl.ds(HIGH, RIM)], (c, xm, y)))
            made.append(
                send(pack.at[pl.ds(RX - RIM, RIM)], landing.at[pl.ds(LOW - RIM, RIM)], (c, xp, y))
            )
        return made

    every = (0, LV)
    first = send_rows(S, 0, 1, every) + send_rows(K, 0, 1, every) + send_packs(PL1, PH1, RL1, RH1)
    levels_copy = send(state.at[0, pl.ds(0, NS)], PART, partner)
    rest = send_corners(PL1, PH1, RL1, RH1) + send_rows(K, 1, RIM - 1, every)

    for peer in neighbours:
        pl.semaphore_signal(near_sem, inc=1, device_id=peer, device_id_type=MESH)

    for copy in local[4:]:
        copy.wait()

    def look_up(r, carry):
        at = pl.ds(pl.multiple_of(r * 8, 8), 8)
        below = pl.ds(pl.multiple_of(r * 8 + LOW, 8), 8)
        kinds = KINDS[at, :]
        found = [jnp.zeros((8, CY), F32) for _ in range(2 + 2 * NS)]
        for p in range(PLANTS):
            hit = kinds == p
            values = [ptab[0, p], ptab[1, p]]
            values += [lw[l, c, p] for l in range(NS)] + [lw[l, 1 - c, p] for l in range(NS)]
            found = [jnp.where(hit, v, f) for v, f in zip(values, found)]
        for t, f in enumerate(found):
            TAB[t, at, :] = f
        own = jnp.zeros((8, CY), F32)
        for l in range(NS):
            s = jnp.concatenate([S[0, l, below, :], S[1, l, below, :]], axis=1)
            own = own + found[2 + l] * s
        OWN[at, :] = own
        return carry

    lax.fori_loop(0, RX // 8, look_up, 0)
    pick_row = lax.broadcasted_iota(jnp.int32, (RX, RX), 0)
    pick_col = lax.broadcasted_iota(jnp.int32, (RX, RX), 1)
    wanted = jnp.zeros((RX, RX), jnp.int32)
    for x in range(RX):
        wanted = jnp.where(pick_row == x, rows[0, x], wanted)
    picker = jnp.where(wanted == pick_col, 1.0, 0.0).astype(F32)

    for copy in first:
        copy.wait_recv()

    row = lax.broadcasted_iota(jnp.int32, (EX, 128), 0)
    row_ok = (
        ((row >= LOW) & (row < HIGH))
        | ((row >= LOW - RIM) & (row < LOW) & (gx > 0))
        | ((row >= HIGH) & (row < HIGH + RIM) & (gx < 7))
    )

    def clean_packs(from_low, from_high, spans):
        for span in spans:
            ok = row_ok[span]
            from_low[span, :] = jnp.where(ok & (gy > 0), from_low[span, :], 0.0)
            from_high[span, :] = jnp.where(ok & (gy < 7), from_high[span, :], 0.0)

    def clear_rows(ref, tiles, skip, width, levels):
        begin, count = levels
        blank_rows = jnp.zeros((count, width, 128), F32)

        @pl.when(gx == 0)
        def _():
            for t in range(tiles):
                ref[t, begin : begin + count, LOW - skip - width : LOW - skip, :] = blank_rows

        @pl.when(gx == 7)
        def _():
            for t in range(tiles):
                ref[t, begin : begin + count, HIGH + skip : HIGH + skip + width, :] = blank_rows

    clean_packs(RL1, RH1, (OWN_ROWS,))
    clear_rows(S, 2, 0, 1, every)
    clear_rows(K, 2, 0, 1, every)

    def lanes_of(rows):
        return lax.broadcasted_iota(jnp.int32, (rows.stop - rows.start, 128), 1)

    def fill_rim(ref, from_low, from_high, rows, levels):
        lane_at = lanes_of(rows)
        for l in range(levels[0], levels[0] + levels[1]):
            right = pltpu.roll(from_high[rows, :], (128 - RIM * l) % 128, 1)
            left = pltpu.roll(from_low[rows, :], (125 - RIM * l) % 128, 1)
            ref[2, l, rows, :] = jnp.where(
                lane_at < RIM, right, jnp.where(lane_at >= 128 - RIM, left, 0.0)
            )

    wide = slice(LOW - RIM, HIGH + RIM)
    near = slice(LOW - 2, HIGH + 2)
    lane_near = lanes_of(near)

    def vertical(t, l, rows):
        if l == 0:
            total = K[t, 0, rows, :]
        elif l == LV:
            total = K[t, LV - 1, rows, :]
        else:
            total = K[t, l - 1, rows, :] + K[t, l, rows, :]
        KZ[t, l, rows, :] = 0.5 * total

    def along_rows(t, l, rows):
        KX[t, l, rows, :] = 0.5 * (K[t, l, rows, :] + K[t, l, shifted(rows, 1), :])

    def flow(ref, l, t, x, rows, right, left):
        total = KX[t, l, rows, :] * (x - ref[t, l, shifted(rows, 1), :])
        before = shifted(rows, -1)
        total = total + KX[t, l, before, :] * (x - ref[t, l, before, :])
        total = total + KY[t, l, rows, :] * (x - right)
        total = total + KYM[t, l, rows, :] * (x - left)
        up = x if l == LV - 1 else x - ref[t, l + 1, rows, :]
        down = x if l == 0 else x - ref[t, l - 1, rows, :]
        return total + (KZ[t, l + 1, rows, :] * up + KZ[t, l, rows, :] * down)

    first_lane, last_lane = lane == 0, lane == 127

    def beside(values, beyond, before, t):
        to_low = [pltpu.roll(x, 127, 1) for x in values] + [beyond]
        to_high = [pltpu.roll(x, 1, 1) for x in values] + [before]
        right = jnp.where(last_lane, to_low[t + 1], to_low[t])
        left = jnp.where(first_lane, to_high[(t + 2) % 3], to_high[t])
        return right, left

    def residual(l, start):
        k = [K[t, l, OWN_ROWS, :] for t in range(2)]
        s = [S[t, l, OWN_ROWS, :] for t in range(2)]
        k_beyond = pltpu.roll(RH1[OWN_ROWS, :], (127 - RIM * l) % 128, 1)
        k_before = pltpu.roll(RL1[OWN_ROWS, :], (126 - RIM * l) % 128, 1)
        s_beyond = pltpu.roll(RH1[OWN_ROWS, :], 31 - l, 1)
        s_before = pltpu.roll(RL1[OWN_ROWS, :], 32 - l, 1)
        for t in range(2):
            if l == start:
                vertical(t, l, OWN_ROWS)
            if l + 1 != NS or start == NS:
                vertical(t, l + 1, OWN_ROWS)
            along_rows(t, l, slice(LOW - 1, HIGH))
            right, left = beside(k, k_beyond, k_before, t)
            KY[t, l, OWN_ROWS, :] = 0.5 * (k[t] + right)
            KYM[t, l, OWN_ROWS, :] = 0.5 * (k[t] + left)
            right, left = beside(s, s_beyond, s_before, t)
            Q0[t, l, OWN_ROWS, :] = -flow(S, l, t, s[t], OWN_ROWS, right, left)

    def send_basis(levels, pack_low, pack_high, from_low, from_high):
        low, high = blank, blank
        for l in range(levels[0], levels[0] + levels[1]):
            low, high = edges(Q0[0, l, OWN_ROWS, :], Q0[1, l, OWN_ROWS, :], l, low, high)
        pack_low[...] = low
        pack_high[...] = high
        packs = (pack_low, pack_high, from_low, from_high)
        return send_corners(*packs) + send_rows(Q0, 0, RIM, levels) + send_packs(*packs)

    for l in range(NS, LV):
        residual(l, NS)
    deep = (NS, LV - NS)
    deep_copies = send_basis(deep, PL2, PH2, RL2, RH2)
    pl.semaphore_wait(near_sem, len(neighbours))
    for i, j in ring:
        pl.semaphore_signal(far_sem, inc=1, device_id=at_offset(2 * i, 2 * j), device_id_type=MESH)
    for l in range(NS):
        residual(l, 0)

    levels_copy.wait_recv()
    received = PART[...].reshape(NS * RX, CY)
    mixed = jnp.concatenate(
        [
            lax.dot_general(
                received[:, b : b + PATCH],
                RW[b : b + PATCH, :],
                (((1,), (1,)), ((), ())),
                precision=HP,
                preferred_element_type=F32,
            )
            for b in range(0, CY, PATCH)
        ],
        axis=1,
    )
    other = jnp.zeros((RX, CY), F32)
    for l in range(NS):
        remapped = jnp.dot(
            picker, mixed[l * RX : (l + 1) * RX], precision=HP, preferred_element_type=F32
        )
        other = other + TAB[2 + NS + l] * remapped
    own = OWN[...]
    is_air = c == 0
    air = jnp.where(is_air, own, other)
    soil = jnp.where(is_air, other, own)
    flux = TAB[0] * (TAB[1] * soil - air)
    FLUX[...] = flux
    results = [pltpu.make_async_copy(FLUX, flux_out.at[0], lsem.at[9])]
    results[0].start()
    signed = jnp.where(is_air, flux, -flux)
    for l in range(NS):
        top = signed * TAB[2 + l]
        if l == 0:
            top = top + SURF[...]
        for t in range(2):
            Q0[t, l, OWN_ROWS, :] = Q0[t, l, OWN_ROWS, :] + top[:, 128 * t : 128 * t + 128]

    coupled = (0, NS)
    coupled_copies = send_basis(coupled, PL3, PH3, RL3, RH3)

    for copy in rest:
        copy.wait_recv()
    clean_packs(RL1, RH1, (slice(0, LOW), slice(HIGH, EX)))
    clear_rows(K, 2, 1, RIM - 1, every)
    fill_rim(K, RL1, RH1, wide, every)
    for l in range(LV + 1):
        for rows in (slice(LOW - 2, LOW), slice(HIGH, HIGH + 2)):
            for t in range(2):
                vertical(t, l, rows)
        vertical(2, l, near)
        if l == LV:
            break
        for t in range(2):
            along_rows(t, l, slice(LOW - 3, LOW - 1))
            along_rows(t, l, slice(HIGH, HIGH + 2))
        along_rows(2, l, slice(LOW - 3, HIGH + 2))
        for rows, tiles in ((slice(LOW - 2, LOW), (0, 1)), (slice(HIGH, HIGH + 2), (0, 1)), (near, (2,))):
            lane_at = lanes_of(rows)
            k = [K[t, l, rows, :] for t in range(TILES)]
            for t in tiles:
                beyond, before = pltpu.roll(k[(t + 1) % 3], 127, 1), pltpu.roll(k[(t + 2) % 3], 1, 1)
                right = jnp.where(lane_at == 127, beyond, pltpu.roll(k[t], 127, 1))
                left = jnp.where(lane_at == 0, before, pltpu.roll(k[t], 1, 1))
                KY[t, l, rows, :] = 0.5 * (k[t] + right)
                KYM[t, l, rows, :] = 0.5 * (k[t] + left)

    def land_basis(copies, levels, from_low, from_high):
        for copy in copies:
            copy.wait_recv()
        clean_packs(from_low, from_high, (slice(0, EX),))
        clear_rows(Q0, 2, 0, RIM, levels)
        fill_rim(Q0, from_low, from_high, wide, levels)

    shift = storage[0, 0]
    scale = 1.0 / SHIFT

    def apply(q_ref, rows, tiles, emit, begin, end):
        lane_at = lanes_of(rows)
        for l in range(begin, end):
            x = [q_ref[t, l, rows, :] for t in range(TILES)]
            to_low = [pltpu.roll(v, 127, 1) for v in x]
            to_high = [pltpu.roll(v, 1, 1) for v in x]
            for t in range(tiles):
                right = jnp.where(lane_at == 127, to_low[(t + 1) % 3], to_low[t])
                left = jnp.where(lane_at == 0, to_high[(t + 2) % 3], to_high[t])
                emit(l, t, x[t], flow(q_ref, l, t, x[t], rows, right, left), rows)

    rim_ok = ((lane_near < RIM) & (gy < 7)) | ((lane_near >= 128 - RIM) & (gy > 0))
    rim_mask = jnp.where(rim_ok, 1.0, 0.0).astype(F32)

    def emit0(l, t, x, total, rows):
        q = total * scale - x
        if t < 2:
            W0[t, l, rows, :] = shift * x + total
        else:
            q = q * rim_mask
        Q1[t, l, rows, :] = q

    def emit1(l, t, x, total, rows):
        q = 2.0 * (total * scale - x) - Q0[t, l, rows, :]
        if t < 2:
            W1[t, l, rows, :] = shift * x + total
        else:
            q = q * rim_mask[0 : rows.stop - rows.start]
        Q2[t, l, rows, :] = q

    sums = [jnp.zeros((8, 128), F32) for _ in range(9)]

    def emit2(l, t, x, total, rows):
        w2 = shift * x + total
        w0, w1, q0 = W0[t, l, rows, :], W1[t, l, rows, :], Q0[t, l, rows, :]
        products = (w0 * q0, w0 * w0, w1 * q0, w1 * w0, w1 * w1, w2 * q0, w2 * w0, w2 * w1, w2 * w2)
        for i, product in enumerate(products):
            sums[i] = sums[i] + fold(product)

    def applications(begin, end):
        step = 1 if begin else 0
        apply(Q0, near, TILES, emit0, begin, end)
        clear_rows(Q1, TILES, 0, 2, (begin, end - begin))
        more = 0 if begin else 1
        begin, end = begin + step, end + more
        apply(Q1, slice(LOW - 1, HIGH + 1), TILES, emit1, begin, end)
        clear_rows(Q2, TILES, 0, 1, (begin, end - begin))
        begin, end = begin + step, end + more
        apply(Q2, OWN_ROWS, 2, emit2, begin, end)

    land_basis(deep_copies, deep, RL2, RH2)
    applications(NS + 1, LV)
    land_basis(coupled_copies, coupled, RL3, RH3)
    applications(0, NS + 1)

    one_lane = lax.broadcasted_iota(jnp.int32, (1, 128), 1)
    packed = jnp.zeros((1, 128), F32)
    for i, part in enumerate(sums):
        packed = jnp.where(one_lane == i, jnp.sum(part, keepdims=True), packed)
    me = gx * 8 + gy
    ROW[0:1, :] = packed
    GATH[pl.ds(me, 1), :] = packed
    pl.semaphore_wait(far_sem, len(ring))
    for peer in peers:
        pltpu.make_async_remote_copy(
            src_ref=ROW.at[pl.ds(0, 1)],
            dst_ref=GATH.at[pl.ds(me, 1)],
            send_sem=lsem.at[7],
            recv_sem=lsem.at[8],
            device_id=peer,
            device_id_type=MESH,
        ).start()
    all_rows = GATH.at[pl.ds(0, len(peers))]
    pltpu.make_async_copy(all_rows, all_rows, lsem.at[8]).wait()
    totals = jnp.sum(GATH[...], axis=0, keepdims=True)
    def at(i):
        return jnp.sum(jnp.where(one_lane == i, totals, 0.0), axis=1, keepdims=True)

    b0, m00, b1, m01, m11, b2, m02, m12, m22 = [at(i) for i in range(9)]
    l10, l20 = m01 / m00, m02 / m00
    d1 = m11 - m01 * l10
    e1 = m12 - m02 * l10
    l21 = e1 / d1
    d2 = m22 - m02 * l20 - e1 * l21
    z1 = b1 - l10 * b0
    z2 = b2 - l20 * b0 - l21 * z1
    y2 = z2 / d2
    y1 = z1 / d1 - l21 * y2
    y0 = b0 / m00 - l10 * y1 - l20 * y2

    for l in range(LV):
        for t in range(2):
            NEW[l, :, 128 * t : 128 * t + 128] = (
                S[t, l, OWN_ROWS, :]
                + y0 * Q0[t, l, OWN_ROWS, :]
                + y1 * Q1[t, l, OWN_ROWS, :]
                + y2 * Q2[t, l, OWN_ROWS, :]
            )
        if l % 6 == 5:
            done = pl.ds(l - 5, 6)
            results.append(
                pltpu.make_async_copy(NEW.at[done], out.at[0, done], lsem.at[9 + len(results)])
            )
            results[-1].start()
    pltpu.make_async_copy(all_rows, all_rows, lsem.at[7]).wait()
    for copy in sends:
        copy.wait_send()
    for copy in results:
        copy.wait()


def deliver(fields, flux, fields_out, flux_out, held, held_flux, sem_in, sem_out):
    thirds = [pl.ds(i * (LV // 3), LV // 3) for i in range(3)]
    copies = [(fields.at[0, at], held.at[at], fields_out.at[0, at]) for at in thirds]
    copies.append((flux, held_flux, flux_out))
    into = [pltpu.make_async_copy(a, b, sem_in.at[i]) for i, (a, b, _) in enumerate(copies)]
    back = [pltpu.make_async_copy(b, c, sem_out.at[i]) for i, (_, b, c) in enumerate(copies)]
    for copy in into:
        copy.start()
    for arrived, copy in zip(into, back):
        arrived.wait()
        copy.start()
    for copy in back:
        copy.wait()


def body(state, conduct, storage, surface, kinds, ptab, lw, rows, rw):
    hbm = pl.BlockSpec(memory_space=pltpu.HBM)
    smem = pl.BlockSpec(memory_space=pltpu.SMEM)
    field = pltpu.VMEM((TILES, LV, EX, 128), F32)
    inner = pltpu.VMEM((2, LV, EX, 128), F32)
    plane = pltpu.VMEM((RX, CY), F32)
    pack = pltpu.VMEM((RX, 128), F32)
    landing = pltpu.VMEM((EX, 128), F32)
    shapes = (
        jax.ShapeDtypeStruct((1, LV, RX, CY), F32),
        jax.ShapeDtypeStruct((1, RX, CY), F32),
    )
    fields, flux = pl.pallas_call(
        kernel,
        out_shape=shapes,
        in_specs=[hbm, hbm, smem, hbm, hbm, smem, smem, smem, hbm],
        out_specs=(hbm, hbm),
        scratch_shapes=[
            inner,
            field,
            field,
            field,
            field,
            pltpu.VMEM((TILES, LV + 1, EX, 128), F32),
            field,
            field,
            field,
            inner,
            inner,
            pltpu.VMEM((NS, RX, CY), F32),
            plane,
            pltpu.VMEM((RX, CY), jnp.int32),
            pltpu.VMEM((CY, PATCH), F32),
            pltpu.VMEM((2 + 2 * NS, RX, CY), F32),
            plane,
            pack,
            pack,
            landing,
            landing,
            pack,
            pack,
            landing,
            landing,
            pack,
            pack,
            landing,
            landing,
            pltpu.VMEM((8, 128), F32),
            pltpu.VMEM((64, 128), F32),
            pltpu.VMEM((LV, RX, CY), F32),
            plane,
            pltpu.SemaphoreType.DMA((16,)),
            pltpu.SemaphoreType.DMA((32,)),
            pltpu.SemaphoreType.DMA((32,)),
            pltpu.SemaphoreType.REGULAR,
            pltpu.SemaphoreType.REGULAR,
        ],
        compiler_params=pltpu.CompilerParams(
            collective_id=0, has_side_effects=True, vmem_limit_bytes=66_000_000
        ),
    )(state, conduct, storage.reshape(1, 1), surface, kinds, ptab.T, jnp.transpose(lw, (2, 0, 1)), rows, rw)
    return pl.pallas_call(
        deliver,
        out_shape=shapes,
        in_specs=[hbm, hbm],
        out_specs=(hbm, hbm),
        scratch_shapes=[
            pltpu.VMEM((LV, RX, CY), F32),
            pltpu.VMEM((1, RX, CY), F32),
            pltpu.SemaphoreType.DMA((4,)),
            pltpu.SemaphoreType.DMA((4,)),
        ],
        compiler_params=pltpu.CompilerParams(vmem_limit_bytes=66_000_000),
    )(fields, flux)


def solution(mesh):
    in_specs = (
        P("comp", None, "gx", "gy"),
        P("comp", None, "gx", "gy"),
        P("comp"),
        P("comp", "gx", "gy"),
        P("comp", "gx", "gy"),
        P(),
        P(),
        P("comp", "gx"),
        P("comp", "gy", None),
    )
    out_specs = (P("comp", None, "gx", "gy"), P("comp", "gx", "gy"))
    return jax.shard_map(body, mesh=mesh, in_specs=in_specs, out_specs=out_specs, check_vma=False)
```

```python
import jax
import jax.numpy as jnp
from jax import lax
from jax.experimental import pallas as pl
from jax.experimental.pallas import tpu as pltpu
from jax.sharding import PartitionSpec as P

MESH = pl.DeviceIdType.MESH
F32 = jnp.float32
NS = 6
PATCH = 128
PLANTS = 16
LV = 30
RX = 32
CY = 256
RIM = 3
TILES = 3
EX = 48
LOW, HIGH = 8, 40
OWN_ROWS = slice(LOW, HIGH)
INNER = slice(LOW + 4, HIGH - 4)
EDGE = 96
SHIFT = 7.0
HP = lax.Precision.HIGHEST


def shifted(rows, by):
    return slice(rows.start + by, rows.stop + by)


def far_first():
    offsets = []
    for dx in range(4):
        for dh in range(2):
            for dz in range(4):
                for co in range(2):
                    if (dx, dh, dz, co) != (0, 0, 0, 0):
                        hops = min(dx, 4 - dx) + 2 * dh + min(dz, 4 - dz)
                        offsets.append((hops, co, dx, dh, dz))
    return [(dx, dh, dz, co) for _, co, dx, dh, dz in sorted(offsets, reverse=True)]


def kernel(
    state,
    conduct,
    storage,
    surface,
    kinds_in,
    ptab,
    lw,
    rows,
    rw_in,
    out,
    flux_out,
    S,
    K,
    KX,
    KY,
    KYM,
    KZ,
    Q0,
    Q1,
    Q2,
    W0,
    W1,
    PART,
    SURF,
    KINDS,
    RW,
    TAB,
    OWN,
    PL1,
    PH1,
    RL1,
    RH1,
    PL2,
    PH2,
    RL2,
    RH2,
    PL3,
    PH3,
    RL3,
    RH3,
    ROW,
    GATH,
    NEW,
    FLUX,
    lsem,
    ssem,
    rsem,
    near_sem,
    far_sem,
):
    c, gx, gy = lax.axis_index("comp"), lax.axis_index("gx"), lax.axis_index("gy")
    xp, xm = lax.rem(gx + 1, 8), lax.rem(gx + 7, 8)
    yp, ym = lax.rem(gy + 1, 8), lax.rem(gy + 7, 8)
    partner = (1 - c, gx, gy)

    local = []
    for src, dst in ((state, S), (conduct, K)):
        for t in range(2):
            local.append(
                pltpu.make_async_copy(
                    src.at[0, :, :, pl.ds(128 * t, 128)],
                    dst.at[t, :, pl.ds(LOW, RX), :],
                    lsem.at[len(local)],
                )
            )
    for src, dst in ((surface, SURF), (kinds_in, KINDS), (rw_in, RW)):
        local.append(pltpu.make_async_copy(src.at[0], dst, lsem.at[len(local)]))
    for copy in local:
        copy.start()

    peers = [
        (
            c,
            lax.rem(gx // 2 + dx, 4) * 2 + lax.rem(gx + dh, 2),
            lax.rem(gy // 2 + dz, 4) * 2 + lax.rem(gy + co, 2),
        )
        for dx, dh, dz, co in far_first()
    ]
    barrier = pltpu.get_barrier_semaphore()
    def at_offset(i, j):
        return (c, lax.rem(gx + 8 + i, 8), lax.rem(gy + 8 + j, 8))

    neighbours = [at_offset(i, j) for i, j in ((1, 0), (-1, 0), (0, 1), (0, -1))]
    for peer in neighbours + [partner]:
        pl.semaphore_signal(barrier, inc=1, device_id=peer, device_id_type=MESH)

    for copy in local[:4]:
        copy.wait()
    lane = lax.broadcasted_iota(jnp.int32, (RX, 128), 1)
    blank = jnp.zeros((RX, 128), F32)

    def edges(value0, value1, l, low, high):
        own = (lane >= RIM * l) & (lane < RIM * l + RIM)
        low = jnp.where(own, pltpu.roll(value0, RIM * l, 1), low)
        high = jnp.where(own, pltpu.roll(value1, RIM * l + RIM, 1), high)
        return low, high

    low, high = blank, blank
    for l in range(LV):
        s = [S[t, l, OWN_ROWS, :] for t in range(2)]
        k = [K[t, l, OWN_ROWS, :] * (1.0 + 0.5 * jnp.tanh(s[t])) for t in range(2)]
        for t in range(2):
            K[t, l, OWN_ROWS, :] = k[t]
        low, high = edges(k[0], k[1], l, low, high)
        own = lane == EDGE + l
        low = jnp.where(own, pltpu.roll(s[0], EDGE + l, 1), low)
        high = jnp.where(own, pltpu.roll(s[1], EDGE + 1 + l, 1), high)
    PL1[...] = low
    PH1[...] = high

    pl.semaphore_wait(barrier, len(neighbours) + 1)

    sends = []

    def send(src, dst, device):
        i = len(sends)
        copy = pltpu.make_async_remote_copy(
            src_ref=src,
            dst_ref=dst,
            send_sem=ssem.at[i],
            recv_sem=rsem.at[i],
            device_id=device,
            device_id_type=MESH,
        )
        copy.start()
        sends.append(copy)
        return copy

    own_tiles = pl.ds(0, 2)

    def send_rows(ref, skip, width, levels):
        at, n = pl.ds(*levels), pl.ds
        return [
            send(
                ref.at[own_tiles, at, n(LOW + skip, width), :],
                ref.at[own_tiles, at, n(HIGH + skip, width), :],
                (c, xm, gy),
            ),
            send(
                ref.at[own_tiles, at, n(HIGH - skip - width, width), :],
                ref.at[own_tiles, at, n(LOW - skip - width, width), :],
                (c, xp, gy),
            ),
        ]

    def send_packs(low_pack, high_pack, from_low, from_high):
        return [
            send(low_pack, from_high.at[pl.ds(LOW, RX)], (c, gx, ym)),
            send(high_pack, from_low.at[pl.ds(LOW, RX)], (c, gx, yp)),
        ]

    def send_corners(low_pack, high_pack, from_low, from_high):
        made = []
        for pack, landing, y in ((low_pack, from_high, ym), (high_pack, from_low, yp)):
            made.append(send(pack.at[pl.ds(0, RIM)], landing.at[pl.ds(HIGH, RIM)], (c, xm, y)))
            made.append(
                send(pack.at[pl.ds(RX - RIM, RIM)], landing.at[pl.ds(LOW - RIM, RIM)], (c, xp, y))
            )
        return made

    every = (0, LV)
    first = send_rows(S, 0, 1, every) + send_rows(K, 0, 1, every) + send_packs(PL1, PH1, RL1, RH1)
    levels_copy = send(state.at[0, pl.ds(0, NS)], PART, partner)
    rest = send_rows(K, 1, RIM - 1, every)

    for copy in local[4:]:
        copy.wait()

    def look_up(r, carry):
        at = pl.ds(pl.multiple_of(r * 8, 8), 8)
        below = pl.ds(pl.multiple_of(r * 8 + LOW, 8), 8)
        kinds = KINDS[at, :]
        found = [jnp.zeros((8, CY), F32) for _ in range(2 + 2 * NS)]
        for p in range(PLANTS):
            hit = kinds == p
            values = [ptab[0, p], ptab[1, p]]
            values += [lw[l, c, p] for l in range(NS)] + [lw[l, 1 - c, p] for l in range(NS)]
            found = [jnp.where(hit, v, f) for v, f in zip(values, found)]
        for t, f in enumerate(found):
            TAB[t, at, :] = f
        own = jnp.zeros((8, CY), F32)
        for l in range(NS):
            s = jnp.concatenate([S[0, l, below, :], S[1, l, below, :]], axis=1)
            own = own + found[2 + l] * s
        OWN[at, :] = own
        return carry

    lax.fori_loop(0, RX // 8, look_up, 0)
    pick_row = lax.broadcasted_iota(jnp.int32, (RX, RX), 0)
    pick_col = lax.broadcasted_iota(jnp.int32, (RX, RX), 1)
    wanted = jnp.zeros((RX, RX), jnp.int32)
    for x in range(RX):
        wanted = jnp.where(pick_row == x, rows[0, x], wanted)
    picker = jnp.where(wanted == pick_col, 1.0, 0.0).astype(F32)

    for copy in first:
        copy.wait_recv()

    near_ring = [(i, j) for i in range(-2, 3) for j in range(-2, 3) if abs(i) + abs(j) == 2]
    far_ring = [(4, 0), (0, 4), (2, 2), (2, -2), (-2, 2), (-2, -2)]
    rest += send_corners(PL1, PH1, RL1, RH1)
    for i, j in near_ring:
        pl.semaphore_signal(near_sem, inc=1, device_id=at_offset(i, j), device_id_type=MESH)

    row = lax.broadcasted_iota(jnp.int32, (EX, 128), 0)
    row_ok = (
        ((row >= LOW) & (row < HIGH))
        | ((row >= LOW - RIM) & (row < LOW) & (gx > 0))
        | ((row >= HIGH) & (row < HIGH + RIM) & (gx < 7))
    )

    def clean_packs(from_low, from_high, spans):
        for span in spans:
            ok = row_ok[span]
            from_low[span, :] = jnp.where(ok & (gy > 0), from_low[span, :], 0.0)
            from_high[span, :] = jnp.where(ok & (gy < 7), from_high[span, :], 0.0)

    def clear_rows(ref, tiles, skip, width, levels):
        begin, count = levels
        blank_rows = jnp.zeros((count, width, 128), F32)

        @pl.when(gx == 0)
        def _():
            for t in range(tiles):
                ref[t, begin : begin + count, LOW - skip - width : LOW - skip, :] = blank_rows

        @pl.when(gx == 7)
        def _():
            for t in range(tiles):
                ref[t, begin : begin + count, HIGH + skip : HIGH + skip + width, :] = blank_rows

    clean_packs(RL1, RH1, (OWN_ROWS,))
    clear_rows(S, 2, 0, 1, every)
    clear_rows(K, 2, 0, 1, every)

    def lanes_of(rows):
        return lax.broadcasted_iota(jnp.int32, (rows.stop - rows.start, 128), 1)

    def fill_rim(ref, from_low, from_high, rows, levels):
        lane_at = lanes_of(rows)
        for l in range(levels[0], levels[0] + levels[1]):
            right = pltpu.roll(from_high[rows, :], (128 - RIM * l) % 128, 1)
            left = pltpu.roll(from_low[rows, :], (125 - RIM * l) % 128, 1)
            ref[2, l, rows, :] = jnp.where(
                lane_at < RIM, right, jnp.where(lane_at >= 128 - RIM, left, 0.0)
            )

    wide = slice(LOW - RIM, HIGH + RIM)
    near = slice(LOW - 2, HIGH + 2)
    lane_near = lanes_of(near)

    def vertical(t, l, rows):
        if l == 0:
            total = K[t, 0, rows, :]
        elif l == LV:
            total = K[t, LV - 1, rows, :]
        else:
            total = K[t, l - 1, rows, :] + K[t, l, rows, :]
        KZ[t, l, rows, :] = 0.5 * total

    def along_rows(t, l, rows):
        KX[t, l, rows, :] = 0.5 * (K[t, l, rows, :] + K[t, l, shifted(rows, 1), :])

    def flow(ref, l, t, x, rows, right, left):
        total = KX[t, l, rows, :] * (x - ref[t, l, shifted(rows, 1), :])
        before = shifted(rows, -1)
        total = total + KX[t, l, before, :] * (x - ref[t, l, before, :])
        total = total + KY[t, l, rows, :] * (x - right)
        total = total + KYM[t, l, rows, :] * (x - left)
        up = x if l == LV - 1 else x - ref[t, l + 1, rows, :]
        down = x if l == 0 else x - ref[t, l - 1, rows, :]
        return total + (KZ[t, l + 1, rows, :] * up + KZ[t, l, rows, :] * down)

    first_lane, last_lane = lane == 0, lane == 127

    def beside(values, beyond, before, t):
        to_low = [pltpu.roll(x, 127, 1) for x in values] + [beyond]
        to_high = [pltpu.roll(x, 1, 1) for x in values] + [before]
        right = jnp.where(last_lane, to_low[t + 1], to_low[t])
        left = jnp.where(first_lane, to_high[(t + 2) % 3], to_high[t])
        return right, left

    def residual(l, start):
        k = [K[t, l, OWN_ROWS, :] for t in range(2)]
        s = [S[t, l, OWN_ROWS, :] for t in range(2)]
        k_beyond = pltpu.roll(RH1[OWN_ROWS, :], (127 - RIM * l) % 128, 1)
        k_before = pltpu.roll(RL1[OWN_ROWS, :], (126 - RIM * l) % 128, 1)
        s_beyond = pltpu.roll(RH1[OWN_ROWS, :], 31 - l, 1)
        s_before = pltpu.roll(RL1[OWN_ROWS, :], 32 - l, 1)
        for t in range(2):
            if l == start:
                vertical(t, l, OWN_ROWS)
            if l + 1 != NS or start == NS:
                vertical(t, l + 1, OWN_ROWS)
            along_rows(t, l, slice(LOW - 1, HIGH))
            right, left = beside(k, k_beyond, k_before, t)
            KY[t, l, OWN_ROWS, :] = 0.5 * (k[t] + right)
            KYM[t, l, OWN_ROWS, :] = 0.5 * (k[t] + left)
            right, left = beside(s, s_beyond, s_before, t)
            Q0[t, l, OWN_ROWS, :] = -flow(S, l, t, s[t], OWN_ROWS, right, left)

    def send_basis(levels, pack_low, pack_high, from_low, from_high):
        low, high = blank, blank
        for l in range(levels[0], levels[0] + levels[1]):
            low, high = edges(Q0[0, l, OWN_ROWS, :], Q0[1, l, OWN_ROWS, :], l, low, high)
        pack_low[...] = low
        pack_high[...] = high
        packs = (pack_low, pack_high, from_low, from_high)
        return send_corners(*packs) + send_rows(Q0, 0, RIM, levels) + send_packs(*packs)

    for l in range(NS, LV):
        residual(l, NS)
    deep = (NS, LV - NS)
    deep_copies = send_basis(deep, PL2, PH2, RL2, RH2)
    for l in range(NS):
        residual(l, 0)

    levels_copy.wait_recv()
    received = PART[...].reshape(NS * RX, CY)
    mixed = jnp.concatenate(
        [
            lax.dot_general(
                received[:, b : b + PATCH],
                RW[b : b + PATCH, :],
                (((1,), (1,)), ((), ())),
                precision=HP,
                preferred_element_type=F32,
            )
            for b in range(0, CY, PATCH)
        ],
        axis=1,
    )
    other = jnp.zeros((RX, CY), F32)
    for l in range(NS):
        remapped = jnp.dot(
            picker, mixed[l * RX : (l + 1) * RX], precision=HP, preferred_element_type=F32
        )
        other = other + TAB[2 + NS + l] * remapped
    own = OWN[...]
    is_air = c == 0
    air = jnp.where(is_air, own, other)
    soil = jnp.where(is_air, other, own)
    flux = TAB[0] * (TAB[1] * soil - air)
    FLUX[...] = flux
    results = [pltpu.make_async_copy(FLUX, flux_out.at[0], lsem.at[9])]
    results[0].start()
    signed = jnp.where(is_air, flux, -flux)
    for l in range(NS):
        top = signed * TAB[2 + l]
        if l == 0:
            top = top + SURF[...]
        for t in range(2):
            Q0[t, l, OWN_ROWS, :] = Q0[t, l, OWN_ROWS, :] + top[:, 128 * t : 128 * t + 128]

    coupled = (0, NS)
    coupled_copies = send_basis(coupled, PL3, PH3, RL3, RH3)
    pl.semaphore_wait(near_sem, len(near_ring))
    for i, j in far_ring:
        pl.semaphore_signal(far_sem, inc=1, device_id=at_offset(i, j), device_id_type=MESH)

    low_rim, high_rim = slice(LOW - RIM, LOW), slice(HIGH, HIGH + RIM)

    def beside_pairs(l, rows, tiles):
        lane_at = lanes_of(rows)
        k = [K[t, l, rows, :] for t in range(TILES)]
        for t in tiles:
            beyond, before = pltpu.roll(k[(t + 1) % 3], 127, 1), pltpu.roll(k[(t + 2) % 3], 1, 1)
            right = jnp.where(lane_at == 127, beyond, pltpu.roll(k[t], 127, 1))
            left = jnp.where(lane_at == 0, before, pltpu.roll(k[t], 1, 1))
            KY[t, l, rows, :] = 0.5 * (k[t] + right)
            KYM[t, l, rows, :] = 0.5 * (k[t] + left)

    def pairs_right_left():
        fill_rim(K, RL1, RH1, OWN_ROWS, every)
        for l in range(LV + 1):
            vertical(2, l, OWN_ROWS)
            if l < LV:
                along_rows(2, l, slice(LOW, HIGH - 1))
                beside_pairs(l, OWN_ROWS, (2,))

    def pairs_above_below():
        for copy in rest:
            copy.wait_recv()
        clean_packs(RL1, RH1, (slice(0, LOW), slice(HIGH, EX)))
        clear_rows(K, 2, 1, RIM - 1, every)
        fill_rim(K, RL1, RH1, low_rim, every)
        fill_rim(K, RL1, RH1, high_rim, every)
        for l in range(LV + 1):
            for rows in (slice(LOW - 2, LOW), slice(HIGH, HIGH + 2)):
                for t in range(TILES):
                    vertical(t, l, rows)
                if l < LV:
                    beside_pairs(l, rows, range(TILES))
            if l == LV:
                break
            for t in range(2):
                along_rows(t, l, slice(LOW - 3, LOW - 1))
                along_rows(t, l, slice(HIGH, HIGH + 2))
            along_rows(2, l, slice(LOW - 3, LOW))
            along_rows(2, l, slice(HIGH - 1, HIGH + 2))

    def land_columns(copies, levels, from_low, from_high):
        for copy in copies:
            copy.wait_recv()
        clean_packs(from_low, from_high, (OWN_ROWS,))
        fill_rim(Q0, from_low, from_high, OWN_ROWS, levels)

    def land_rows(copies, levels, from_low, from_high):
        for copy in copies:
            copy.wait_recv()
        clean_packs(from_low, from_high, (slice(0, LOW), slice(HIGH, EX)))
        clear_rows(Q0, 2, 0, RIM, levels)
        fill_rim(Q0, from_low, from_high, low_rim, levels)
        fill_rim(Q0, from_low, from_high, high_rim, levels)

    shift = storage[0, 0]
    scale = 1.0 / SHIFT

    def apply(q_ref, rows, tiles, emit, begin, end):
        lane_at = lanes_of(rows)
        for l in range(begin, end):
            x = [q_ref[t, l, rows, :] for t in range(TILES)]
            to_low = [pltpu.roll(v, 127, 1) for v in x]
            to_high = [pltpu.roll(v, 1, 1) for v in x]
            for t in range(tiles):
                right = jnp.where(lane_at == 127, to_low[(t + 1) % 3], to_low[t])
                left = jnp.where(lane_at == 0, to_high[(t + 2) % 3], to_high[t])
                emit(l, t, x[t], flow(q_ref, l, t, x[t], rows, right, left), rows)

    rim_ok = ((lane_near < RIM) & (gy < 7)) | ((lane_near >= 128 - RIM) & (gy > 0))
    rim_mask = jnp.where(rim_ok, 1.0, 0.0).astype(F32)

    def emit0(l, t, x, total, rows):
        q = total * scale - x
        if t < 2:
            W0[t, l, rows, :] = shift * x + total
        else:
            q = q * rim_mask[0 : rows.stop - rows.start]
        Q1[t, l, rows, :] = q

    def emit1(l, t, x, total, rows):
        q = 2.0 * (total * scale - x) - Q0[t, l, rows, :]
        if t < 2:
            W1[t, l, rows, :] = shift * x + total
        else:
            q = q * rim_mask[0 : rows.stop - rows.start]
        Q2[t, l, rows, :] = q

    sums = [jnp.zeros((8, 128), F32) for _ in range(9)]
    edge_sums = [jnp.zeros((4, 128), F32) for _ in range(9)]

    def emit2(l, t, x, total, rows):
        w2 = shift * x + total
        w0, w1, q0 = W0[t, l, rows, :], W1[t, l, rows, :], Q0[t, l, rows, :]
        products = (w0 * q0, w0 * w0, w1 * q0, w1 * w0, w1 * w1, w2 * q0, w2 * w0, w2 * w1, w2 * w2)
        for i, product in enumerate(products):
            if rows == INNER:
                sums[i] = sums[i] + ((product[0:8] + product[8:16]) + product[16:24])
            else:
                edge_sums[i] = edge_sums[i] + product

    def applications(begin, end, inside):
        step, more = (1, 0) if begin else (0, 1)
        if inside:
            passes = ((slice(9, 39),), (slice(10, 38),), (INNER,))
        else:
            passes = (
                (slice(6, 9), slice(39, 42)),
                (slice(7, 10), slice(38, 41)),
                (slice(8, 12), slice(36, 40)),
            )
        for rows in passes[0]:
            apply(Q0, rows, TILES, emit0, begin, end)
        if not inside:
            clear_rows(Q1, TILES, 0, 2, (begin, end - begin))
        begin, end = begin + step, end + more
        for rows in passes[1]:
            apply(Q1, rows, TILES, emit1, begin, end)
        if not inside:
            clear_rows(Q2, TILES, 0, 1, (begin, end - begin))
        begin, end = begin + step, end + more
        for rows in passes[2]:
            apply(Q2, rows, 2, emit2, begin, end)

    pairs_right_left()
    land_columns(deep_copies[-2:], deep, RL2, RH2)
    applications(NS + 1, LV, True)
    land_columns(coupled_copies[-2:], coupled, RL3, RH3)
    applications(0, NS + 1, True)
    pairs_above_below()
    land_rows(deep_copies[:-2], deep, RL2, RH2)
    applications(NS + 1, LV, False)
    land_rows(coupled_copies[:-2], coupled, RL3, RH3)
    applications(0, NS + 1, False)
    sums = [(a[0:4] + a[4:8]) + b for a, b in zip(sums, edge_sums)]

    one_lane = lax.broadcasted_iota(jnp.int32, (1, 128), 1)
    packed = jnp.zeros((1, 128), F32)
    for i, part in enumerate(sums):
        packed = jnp.where(one_lane == i, jnp.sum(part, keepdims=True), packed)
    me = gx * 8 + gy
    ROW[0:1, :] = packed
    GATH[pl.ds(me, 1), :] = packed
    pl.semaphore_wait(far_sem, len(far_ring))
    for peer in peers:
        pltpu.make_async_remote_copy(
            src_ref=ROW.at[pl.ds(0, 1)],
            dst_ref=GATH.at[pl.ds(me, 1)],
            send_sem=lsem.at[7],
            recv_sem=lsem.at[8],
            device_id=peer,
            device_id_type=MESH,
        ).start()
    all_rows = GATH.at[pl.ds(0, len(peers))]
    pltpu.make_async_copy(all_rows, all_rows, lsem.at[8]).wait()
    totals = jnp.sum(GATH[...], axis=0, keepdims=True)
    def at(i):
        return jnp.sum(jnp.where(one_lane == i, totals, 0.0), axis=1, keepdims=True)

    b0, m00, b1, m01, m11, b2, m02, m12, m22 = [at(i) for i in range(9)]
    l10, l20 = m01 / m00, m02 / m00
    d1 = m11 - m01 * l10
    e1 = m12 - m02 * l10
    l21 = e1 / d1
    d2 = m22 - m02 * l20 - e1 * l21
    z1 = b1 - l10 * b0
    z2 = b2 - l20 * b0 - l21 * z1
    y2 = z2 / d2
    y1 = z1 / d1 - l21 * y2
    y0 = b0 / m00 - l10 * y1 - l20 * y2

    for l in range(LV):
        for t in range(2):
            NEW[l, :, 128 * t : 128 * t + 128] = (
                S[t, l, OWN_ROWS, :]
                + y0 * Q0[t, l, OWN_ROWS, :]
                + y1 * Q1[t, l, OWN_ROWS, :]
                + y2 * Q2[t, l, OWN_ROWS, :]
            )
        if l % 6 == 5:
            done = pl.ds(l - 5, 6)
            results.append(
                pltpu.make_async_copy(NEW.at[done], out.at[0, done], lsem.at[9 + len(results)])
            )
            results[-1].start()
    pltpu.make_async_copy(all_rows, all_rows, lsem.at[7]).wait()
    for copy in sends:
        copy.wait_send()
    for copy in results:
        copy.wait()


def deliver(fields, flux, fields_out, flux_out, held, held_flux, sem_in, sem_out):
    thirds = [pl.ds(i * (LV // 3), LV // 3) for i in range(3)]
    copies = [(fields.at[0, at], held.at[at], fields_out.at[0, at]) for at in thirds]
    copies.append((flux, held_flux, flux_out))
    into = [pltpu.make_async_copy(a, b, sem_in.at[i]) for i, (a, b, _) in enumerate(copies)]
    back = [pltpu.make_async_copy(b, c, sem_out.at[i]) for i, (_, b, c) in enumerate(copies)]
    for copy in into:
        copy.start()
    for arrived, copy in zip(into, back):
        arrived.wait()
        copy.start()
    for copy in back:
        copy.wait()


def body(state, conduct, storage, surface, kinds, ptab, lw, rows, rw):
    hbm = pl.BlockSpec(memory_space=pltpu.HBM)
    smem = pl.BlockSpec(memory_space=pltpu.SMEM)
    field = pltpu.VMEM((TILES, LV, EX, 128), F32)
    inner = pltpu.VMEM((2, LV, EX, 128), F32)
    plane = pltpu.VMEM((RX, CY), F32)
    pack = pltpu.VMEM((RX, 128), F32)
    landing = pltpu.VMEM((EX, 128), F32)
    shapes = (
        jax.ShapeDtypeStruct((1, LV, RX, CY), F32),
        jax.ShapeDtypeStruct((1, RX, CY), F32),
    )
    fields, flux = pl.pallas_call(
        kernel,
        out_shape=shapes,
        in_specs=[hbm, hbm, smem, hbm, hbm, smem, smem, smem, hbm],
        out_specs=(hbm, hbm),
        scratch_shapes=[
            inner,
            field,
            field,
            field,
            field,
            pltpu.VMEM((TILES, LV + 1, EX, 128), F32),
            field,
            field,
            field,
            inner,
            inner,
            pltpu.VMEM((NS, RX, CY), F32),
            plane,
            pltpu.VMEM((RX, CY), jnp.int32),
            pltpu.VMEM((CY, PATCH), F32),
            pltpu.VMEM((2 + 2 * NS, RX, CY), F32),
            plane,
            pack,
            pack,
            landing,
            landing,
            pack,
            pack,
            landing,
            landing,
            pack,
            pack,
            landing,
            landing,
            pltpu.VMEM((8, 128), F32),
            pltpu.VMEM((64, 128), F32),
            pltpu.VMEM((LV, RX, CY), F32),
            plane,
            pltpu.SemaphoreType.DMA((16,)),
            pltpu.SemaphoreType.DMA((32,)),
            pltpu.SemaphoreType.DMA((32,)),
            pltpu.SemaphoreType.REGULAR,
            pltpu.SemaphoreType.REGULAR,
        ],
        compiler_params=pltpu.CompilerParams(
            collective_id=0, has_side_effects=True, vmem_limit_bytes=66_000_000
        ),
    )(state, conduct, storage.reshape(1, 1), surface, kinds, ptab.T, jnp.transpose(lw, (2, 0, 1)), rows, rw)
    return pl.pallas_call(
        deliver,
        out_shape=shapes,
        in_specs=[hbm, hbm],
        out_specs=(hbm, hbm),
        scratch_shapes=[
            pltpu.VMEM((LV, RX, CY), F32),
            pltpu.VMEM((1, RX, CY), F32),
            pltpu.SemaphoreType.DMA((4,)),
            pltpu.SemaphoreType.DMA((4,)),
        ],
        compiler_params=pltpu.CompilerParams(vmem_limit_bytes=66_000_000),
    )(fields, flux)


def solution(mesh):
    in_specs = (
        P("comp", None, "gx", "gy"),
        P("comp", None, "gx", "gy"),
        P("comp"),
        P("comp", "gx", "gy"),
        P("comp", "gx", "gy"),
        P(),
        P(),
        P("comp", "gx"),
        P("comp", "gy", None),
    )
    out_specs = (P("comp", None, "gx", "gy"), P("comp", "gx", "gy"))
    return jax.shard_map(body, mesh=mesh, in_specs=in_specs, out_specs=out_specs, check_vma=False)
```

```python
import jax
import jax.numpy as jnp
from jax import lax
from jax.experimental import pallas as pl
from jax.experimental.pallas import tpu as pltpu
from jax.sharding import PartitionSpec as P

MESH = pl.DeviceIdType.MESH
F32 = jnp.float32
NS = 6
PATCH = 128
PLANTS = 16
LV = 30
RX = 32
CY = 256
RIM = 3
TILES = 3
EX = 48
LOW, HIGH = 8, 40
OWN_ROWS = slice(LOW, HIGH)
INNER = slice(LOW + 4, HIGH - 4)
EDGE = 96
SHIFT = 7.0
HP = lax.Precision.HIGHEST


def shifted(rows, by):
    return slice(rows.start + by, rows.stop + by)


def far_first():
    offsets = []
    for dx in range(4):
        for dh in range(2):
            for dz in range(4):
                for co in range(2):
                    if (dx, dh, dz, co) != (0, 0, 0, 0):
                        hops = min(dx, 4 - dx) + 2 * dh + min(dz, 4 - dz)
                        offsets.append((hops, co, dx, dh, dz))
    return [(dx, dh, dz, co) for _, co, dx, dh, dz in sorted(offsets, reverse=True)]


def kernel(
    state,
    conduct,
    storage,
    surface,
    kinds_in,
    ptab,
    lw,
    rows,
    rw_in,
    out,
    flux_out,
    S,
    K,
    KX,
    KY,
    KYM,
    KZ,
    Q0,
    Q1,
    Q2,
    W0,
    W1,
    PART,
    SURF,
    KINDS,
    RW,
    TAB,
    OWN,
    PL1,
    PH1,
    RL1,
    RH1,
    PL2,
    PH2,
    RL2,
    RH2,
    PL3,
    PH3,
    RL3,
    RH3,
    ROW,
    GATH,
    NEW,
    FLUX,
    lsem,
    ssem,
    rsem,
    near_sem,
    far_sem,
):
    c, gx, gy = lax.axis_index("comp"), lax.axis_index("gx"), lax.axis_index("gy")
    xp, xm = lax.rem(gx + 1, 8), lax.rem(gx + 7, 8)
    yp, ym = lax.rem(gy + 1, 8), lax.rem(gy + 7, 8)
    partner = (1 - c, gx, gy)

    local = []
    for src, dst in ((state, S), (conduct, K)):
        for t in range(2):
            local.append(
                pltpu.make_async_copy(
                    src.at[0, :, :, pl.ds(128 * t, 128)],
                    dst.at[t, :, pl.ds(LOW, RX), :],
                    lsem.at[len(local)],
                )
            )
    for src, dst in ((surface, SURF), (kinds_in, KINDS), (rw_in, RW)):
        local.append(pltpu.make_async_copy(src.at[0], dst, lsem.at[len(local)]))
    for copy in local:
        copy.start()

    peers = [
        (
            c,
            lax.rem(gx // 2 + dx, 4) * 2 + lax.rem(gx + dh, 2),
            lax.rem(gy // 2 + dz, 4) * 2 + lax.rem(gy + co, 2),
        )
        for dx, dh, dz, co in far_first()
    ]
    barrier = pltpu.get_barrier_semaphore()
    def at_offset(i, j):
        return (c, lax.rem(gx + 8 + i, 8), lax.rem(gy + 8 + j, 8))

    neighbours = [at_offset(i, j) for i, j in ((1, 0), (-1, 0), (0, 1), (0, -1))]
    for peer in neighbours + [partner]:
        pl.semaphore_signal(barrier, inc=1, device_id=peer, device_id_type=MESH)

    for copy in local[:4]:
        copy.wait()
    lane = lax.broadcasted_iota(jnp.int32, (RX, 128), 1)
    blank = jnp.zeros((RX, 128), F32)

    def edges(value0, value1, l, low, high):
        own = (lane >= RIM * l) & (lane < RIM * l + RIM)
        low = jnp.where(own, pltpu.roll(value0, RIM * l, 1), low)
        high = jnp.where(own, pltpu.roll(value1, RIM * l + RIM, 1), high)
        return low, high

    low, high = blank, blank
    for l in range(LV):
        s = [S[t, l, OWN_ROWS, :] for t in range(2)]
        k = [K[t, l, OWN_ROWS, :] * (1.0 + 0.5 * jnp.tanh(s[t])) for t in range(2)]
        for t in range(2):
            K[t, l, OWN_ROWS, :] = k[t]
        low, high = edges(k[0], k[1], l, low, high)
        own = lane == EDGE + l
        low = jnp.where(own, pltpu.roll(s[0], EDGE + l, 1), low)
        high = jnp.where(own, pltpu.roll(s[1], EDGE + 1 + l, 1), high)
    PL1[...] = low
    PH1[...] = high

    pl.semaphore_wait(barrier, len(neighbours) + 1)

    sends = []

    def send(src, dst, device):
        i = len(sends)
        copy = pltpu.make_async_remote_copy(
            src_ref=src,
            dst_ref=dst,
            send_sem=ssem.at[i],
            recv_sem=rsem.at[i],
            device_id=device,
            device_id_type=MESH,
        )
        copy.start()
        sends.append(copy)
        return copy

    own_tiles = pl.ds(0, 2)

    def send_rows(ref, skip, width, levels):
        at, n = pl.ds(*levels), pl.ds
        return [
            send(
                ref.at[own_tiles, at, n(LOW + skip, width), :],
                ref.at[own_tiles, at, n(HIGH + skip, width), :],
                (c, xm, gy),
            ),
            send(
                ref.at[own_tiles, at, n(HIGH - skip - width, width), :],
                ref.at[own_tiles, at, n(LOW - skip - width, width), :],
                (c, xp, gy),
            ),
        ]

    def send_packs(low_pack, high_pack, from_low, from_high):
        return [
            send(low_pack, from_high.at[pl.ds(LOW, RX)], (c, gx, ym)),
            send(high_pack, from_low.at[pl.ds(LOW, RX)], (c, gx, yp)),
        ]

    def send_corners(low_pack, high_pack, from_low, from_high):
        made = []
        for pack, landing, y in ((low_pack, from_high, ym), (high_pack, from_low, yp)):
            made.append(send(pack.at[pl.ds(0, RIM)], landing.at[pl.ds(HIGH, RIM)], (c, xm, y)))
            made.append(
                send(pack.at[pl.ds(RX - RIM, RIM)], landing.at[pl.ds(LOW - RIM, RIM)], (c, xp, y))
            )
        return made

    every = (0, LV)
    first = send_rows(S, 0, 1, every) + send_rows(K, 0, 1, every) + send_packs(PL1, PH1, RL1, RH1)
    halves = [pl.ds(0, NS // 2), pl.ds(NS // 2, NS // 2)]
    levels_copies = [send(state.at[0, half], PART.at[half], partner) for half in halves]
    rest = send_rows(K, 1, RIM - 1, every)

    for copy in local[4:]:
        copy.wait()

    def look_up(r, carry):
        at = pl.ds(pl.multiple_of(r * 8, 8), 8)
        below = pl.ds(pl.multiple_of(r * 8 + LOW, 8), 8)
        kinds = KINDS[at, :]
        found = [jnp.zeros((8, CY), F32) for _ in range(2 + 2 * NS)]
        for p in range(PLANTS):
            hit = kinds == p
            values = [ptab[0, p], ptab[1, p]]
            values += [lw[l, c, p] for l in range(NS)] + [lw[l, 1 - c, p] for l in range(NS)]
            found = [jnp.where(hit, v, f) for v, f in zip(values, found)]
        for t, f in enumerate(found):
            TAB[t, at, :] = f
        own = jnp.zeros((8, CY), F32)
        for l in range(NS):
            s = jnp.concatenate([S[0, l, below, :], S[1, l, below, :]], axis=1)
            own = own + found[2 + l] * s
        OWN[at, :] = own
        return carry

    lax.fori_loop(0, RX // 8, look_up, 0)
    pick_row = lax.broadcasted_iota(jnp.int32, (RX, RX), 0)
    pick_col = lax.broadcasted_iota(jnp.int32, (RX, RX), 1)
    wanted = jnp.zeros((RX, RX), jnp.int32)
    for x in range(RX):
        wanted = jnp.where(pick_row == x, rows[0, x], wanted)
    picker = jnp.where(wanted == pick_col, 1.0, 0.0).astype(F32)

    for copy in first:
        copy.wait_recv()

    near_ring = [(i, j) for i in range(-2, 3) for j in range(-2, 3) if abs(i) + abs(j) == 2]
    far_ring = [(4, 0), (0, 4), (2, 2), (2, -2), (-2, 2), (-2, -2)]
    rest += send_corners(PL1, PH1, RL1, RH1)
    for i, j in near_ring:
        pl.semaphore_signal(near_sem, inc=1, device_id=at_offset(i, j), device_id_type=MESH)

    row = lax.broadcasted_iota(jnp.int32, (EX, 128), 0)
    row_ok = (
        ((row >= LOW) & (row < HIGH))
        | ((row >= LOW - RIM) & (row < LOW) & (gx > 0))
        | ((row >= HIGH) & (row < HIGH + RIM) & (gx < 7))
    )

    def clean_packs(from_low, from_high, spans):
        for span in spans:
            ok = row_ok[span]
            from_low[span, :] = jnp.where(ok & (gy > 0), from_low[span, :], 0.0)
            from_high[span, :] = jnp.where(ok & (gy < 7), from_high[span, :], 0.0)

    def clear_rows(ref, tiles, skip, width, levels):
        begin, count = levels
        blank_rows = jnp.zeros((count, width, 128), F32)

        @pl.when(gx == 0)
        def _():
            for t in range(tiles):
                ref[t, begin : begin + count, LOW - skip - width : LOW - skip, :] = blank_rows

        @pl.when(gx == 7)
        def _():
            for t in range(tiles):
                ref[t, begin : begin + count, HIGH + skip : HIGH + skip + width, :] = blank_rows

    clean_packs(RL1, RH1, (OWN_ROWS,))
    clear_rows(S, 2, 0, 1, every)
    clear_rows(K, 2, 0, 1, every)

    def lanes_of(rows):
        return lax.broadcasted_iota(jnp.int32, (rows.stop - rows.start, 128), 1)

    def fill_rim(ref, from_low, from_high, rows, levels):
        lane_at = lanes_of(rows)
        for l in range(levels[0], levels[0] + levels[1]):
            right = pltpu.roll(from_high[rows, :], (128 - RIM * l) % 128, 1)
            left = pltpu.roll(from_low[rows, :], (125 - RIM * l) % 128, 1)
            ref[2, l, rows, :] = jnp.where(
                lane_at < RIM, right, jnp.where(lane_at >= 128 - RIM, left, 0.0)
            )

    wide = slice(LOW - RIM, HIGH + RIM)
    near = slice(LOW - 2, HIGH + 2)
    lane_near = lanes_of(near)

    def vertical(t, l, rows):
        if l == 0:
            total = K[t, 0, rows, :]
        elif l == LV:
            total = K[t, LV - 1, rows, :]
        else:
            total = K[t, l - 1, rows, :] + K[t, l, rows, :]
        KZ[t, l, rows, :] = 0.5 * total

    def along_rows(t, l, rows):
        KX[t, l, rows, :] = 0.5 * (K[t, l, rows, :] + K[t, l, shifted(rows, 1), :])

    def flow(ref, l, t, x, rows, right, left):
        total = KX[t, l, rows, :] * (x - ref[t, l, shifted(rows, 1), :])
        before = shifted(rows, -1)
        total = total + KX[t, l, before, :] * (x - ref[t, l, before, :])
        total = total + KY[t, l, rows, :] * (x - right)
        total = total + KYM[t, l, rows, :] * (x - left)
        up = x if l == LV - 1 else x - ref[t, l + 1, rows, :]
        down = x if l == 0 else x - ref[t, l - 1, rows, :]
        return total + (KZ[t, l + 1, rows, :] * up + KZ[t, l, rows, :] * down)

    first_lane, last_lane = lane == 0, lane == 127

    def beside(values, beyond, before, t):
        to_low = [pltpu.roll(x, 127, 1) for x in values] + [beyond]
        to_high = [pltpu.roll(x, 1, 1) for x in values] + [before]
        right = jnp.where(last_lane, to_low[t + 1], to_low[t])
        left = jnp.where(first_lane, to_high[(t + 2) % 3], to_high[t])
        return right, left

    def residual(l, start):
        k = [K[t, l, OWN_ROWS, :] for t in range(2)]
        s = [S[t, l, OWN_ROWS, :] for t in range(2)]
        k_beyond = pltpu.roll(RH1[OWN_ROWS, :], (127 - RIM * l) % 128, 1)
        k_before = pltpu.roll(RL1[OWN_ROWS, :], (126 - RIM * l) % 128, 1)
        s_beyond = pltpu.roll(RH1[OWN_ROWS, :], 31 - l, 1)
        s_before = pltpu.roll(RL1[OWN_ROWS, :], 32 - l, 1)
        for t in range(2):
            if l == start:
                vertical(t, l, OWN_ROWS)
            if l + 1 != NS or start == NS:
                vertical(t, l + 1, OWN_ROWS)
            along_rows(t, l, slice(LOW - 1, HIGH))
            right, left = beside(k, k_beyond, k_before, t)
            KY[t, l, OWN_ROWS, :] = 0.5 * (k[t] + right)
            KYM[t, l, OWN_ROWS, :] = 0.5 * (k[t] + left)
            right, left = beside(s, s_beyond, s_before, t)
            Q0[t, l, OWN_ROWS, :] = -flow(S, l, t, s[t], OWN_ROWS, right, left)

    def send_basis(levels, pack_low, pack_high, from_low, from_high):
        made = send_rows(Q0, 0, RIM, levels)
        low, high = blank, blank
        for l in range(levels[0], levels[0] + levels[1]):
            low, high = edges(Q0[0, l, OWN_ROWS, :], Q0[1, l, OWN_ROWS, :], l, low, high)
        pack_low[...] = low
        pack_high[...] = high
        packs = (pack_low, pack_high, from_low, from_high)
        return made + send_corners(*packs) + send_packs(*packs)

    for l in range(NS, LV):
        residual(l, NS)
    deep = (NS, LV - NS)
    deep_copies = send_basis(deep, PL2, PH2, RL2, RH2)
    for l in range(NS):
        residual(l, 0)

    other = jnp.zeros((RX, CY), F32)
    for h, copy in enumerate(levels_copies):
        copy.wait_recv()
        begin = h * (NS // 2)
        received = PART[begin : begin + NS // 2].reshape(NS // 2 * RX, CY)
        mixed = jnp.concatenate(
            [
                lax.dot_general(
                    received[:, b : b + PATCH],
                    RW[b : b + PATCH, :],
                    (((1,), (1,)), ((), ())),
                    precision=HP,
                    preferred_element_type=F32,
                )
                for b in range(0, CY, PATCH)
            ],
            axis=1,
        )
        for l in range(NS // 2):
            remapped = jnp.dot(
                picker, mixed[l * RX : (l + 1) * RX], precision=HP, preferred_element_type=F32
            )
            other = other + TAB[2 + NS + begin + l] * remapped
    own = OWN[...]
    is_air = c == 0
    air = jnp.where(is_air, own, other)
    soil = jnp.where(is_air, other, own)
    flux = TAB[0] * (TAB[1] * soil - air)
    FLUX[...] = flux
    results = [pltpu.make_async_copy(FLUX, flux_out.at[0], lsem.at[9])]
    results[0].start()
    signed = jnp.where(is_air, flux, -flux)
    for l in range(NS):
        top = signed * TAB[2 + l]
        if l == 0:
            top = top + SURF[...]
        for t in range(2):
            Q0[t, l, OWN_ROWS, :] = Q0[t, l, OWN_ROWS, :] + top[:, 128 * t : 128 * t + 128]

    coupled = (0, NS)
    coupled_copies = send_basis(coupled, PL3, PH3, RL3, RH3)
    pl.semaphore_wait(near_sem, len(near_ring))
    for i, j in far_ring:
        pl.semaphore_signal(far_sem, inc=1, device_id=at_offset(i, j), device_id_type=MESH)

    low_rim, high_rim = slice(LOW - RIM, LOW), slice(HIGH, HIGH + RIM)

    def beside_pairs(l, rows, tiles):
        lane_at = lanes_of(rows)
        k = [K[t, l, rows, :] for t in range(TILES)]
        for t in tiles:
            beyond, before = pltpu.roll(k[(t + 1) % 3], 127, 1), pltpu.roll(k[(t + 2) % 3], 1, 1)
            right = jnp.where(lane_at == 127, beyond, pltpu.roll(k[t], 127, 1))
            left = jnp.where(lane_at == 0, before, pltpu.roll(k[t], 1, 1))
            KY[t, l, rows, :] = 0.5 * (k[t] + right)
            KYM[t, l, rows, :] = 0.5 * (k[t] + left)

    def pairs_right_left():
        fill_rim(K, RL1, RH1, OWN_ROWS, every)
        for l in range(LV + 1):
            vertical(2, l, OWN_ROWS)
            if l < LV:
                along_rows(2, l, slice(LOW, HIGH - 1))
                beside_pairs(l, OWN_ROWS, (2,))

    def pairs_above_below():
        for copy in rest:
            copy.wait_recv()
        clean_packs(RL1, RH1, (slice(0, LOW), slice(HIGH, EX)))
        clear_rows(K, 2, 1, RIM - 1, every)
        fill_rim(K, RL1, RH1, low_rim, every)
        fill_rim(K, RL1, RH1, high_rim, every)
        for l in range(LV + 1):
            for rows in (slice(LOW - 2, LOW), slice(HIGH, HIGH + 2)):
                for t in range(TILES):
                    vertical(t, l, rows)
                if l < LV:
                    beside_pairs(l, rows, range(TILES))
            if l == LV:
                break
            for t in range(2):
                along_rows(t, l, slice(LOW - 3, LOW - 1))
                along_rows(t, l, slice(HIGH, HIGH + 2))
            along_rows(2, l, slice(LOW - 3, LOW))
            along_rows(2, l, slice(HIGH - 1, HIGH + 2))

    def land_columns(copies, levels, from_low, from_high):
        for copy in copies:
            copy.wait_recv()
        clean_packs(from_low, from_high, (OWN_ROWS,))
        fill_rim(Q0, from_low, from_high, OWN_ROWS, levels)

    def land_rows(copies, levels, from_low, from_high):
        for copy in copies:
            copy.wait_recv()
        clean_packs(from_low, from_high, (slice(0, LOW), slice(HIGH, EX)))
        clear_rows(Q0, 2, 0, RIM, levels)
        fill_rim(Q0, from_low, from_high, low_rim, levels)
        fill_rim(Q0, from_low, from_high, high_rim, levels)

    shift = storage[0, 0]
    scale = 1.0 / SHIFT

    def apply(q_ref, rows, tiles, emit, begin, end):
        lane_at = lanes_of(rows)
        for l in range(begin, end):
            x = [q_ref[t, l, rows, :] for t in range(TILES)]
            to_low = [pltpu.roll(v, 127, 1) for v in x]
            to_high = [pltpu.roll(v, 1, 1) for v in x]
            for t in range(tiles):
                right = jnp.where(lane_at == 127, to_low[(t + 1) % 3], to_low[t])
                left = jnp.where(lane_at == 0, to_high[(t + 2) % 3], to_high[t])
                emit(l, t, x[t], flow(q_ref, l, t, x[t], rows, right, left), rows)

    rim_ok = ((lane_near < RIM) & (gy < 7)) | ((lane_near >= 128 - RIM) & (gy > 0))
    rim_mask = jnp.where(rim_ok, 1.0, 0.0).astype(F32)

    def emit0(l, t, x, total, rows):
        q = total * scale - x
        if t < 2:
            W0[t, l, rows, :] = shift * x + total
        else:
            q = q * rim_mask[0 : rows.stop - rows.start]
        Q1[t, l, rows, :] = q

    def emit1(l, t, x, total, rows):
        q = 2.0 * (total * scale - x) - Q0[t, l, rows, :]
        if t < 2:
            W1[t, l, rows, :] = shift * x + total
        else:
            q = q * rim_mask[0 : rows.stop - rows.start]
        Q2[t, l, rows, :] = q

    sums = [jnp.zeros((8, 128), F32) for _ in range(9)]
    edge_sums = [jnp.zeros((4, 128), F32) for _ in range(9)]

    def emit2(l, t, x, total, rows):
        w2 = shift * x + total
        w0, w1, q0 = W0[t, l, rows, :], W1[t, l, rows, :], Q0[t, l, rows, :]
        products = (w0 * q0, w0 * w0, w1 * q0, w1 * w0, w1 * w1, w2 * q0, w2 * w0, w2 * w1, w2 * w2)
        for i, product in enumerate(products):
            if rows == INNER:
                sums[i] = sums[i] + ((product[0:8] + product[8:16]) + product[16:24])
            else:
                edge_sums[i] = edge_sums[i] + product

    def applications(begin, end, inside):
        step, more = (1, 0) if begin else (0, 1)
        if inside:
            passes = ((slice(9, 39),), (slice(10, 38),), (INNER,))
        else:
            passes = (
                (slice(6, 9), slice(39, 42)),
                (slice(7, 10), slice(38, 41)),
                (slice(8, 12), slice(36, 40)),
            )
        for rows in passes[0]:
            apply(Q0, rows, TILES, emit0, begin, end)
        if not inside:
            clear_rows(Q1, TILES, 0, 2, (begin, end - begin))
        begin, end = begin + step, end + more
        for rows in passes[1]:
            apply(Q1, rows, TILES, emit1, begin, end)
        if not inside:
            clear_rows(Q2, TILES, 0, 1, (begin, end - begin))
        begin, end = begin + step, end + more
        for rows in passes[2]:
            apply(Q2, rows, 2, emit2, begin, end)

    pairs_right_left()
    land_columns(deep_copies[-2:], deep, RL2, RH2)
    applications(NS + 1, LV, True)
    land_columns(coupled_copies[-2:], coupled, RL3, RH3)
    applications(0, NS + 1, True)
    pairs_above_below()
    land_rows(deep_copies[:-2], deep, RL2, RH2)
    applications(NS + 1, LV, False)
    land_rows(coupled_copies[:-2], coupled, RL3, RH3)
    applications(0, NS + 1, False)
    sums = [(a[0:4] + a[4:8]) + b for a, b in zip(sums, edge_sums)]

    one_lane = lax.broadcasted_iota(jnp.int32, (1, 128), 1)
    packed = jnp.zeros((1, 128), F32)
    for i, part in enumerate(sums):
        packed = jnp.where(one_lane == i, jnp.sum(part, keepdims=True), packed)
    me = gx * 8 + gy
    ROW[0:1, :] = packed
    GATH[pl.ds(me, 1), :] = packed
    pl.semaphore_wait(far_sem, len(far_ring))
    for peer in peers:
        pltpu.make_async_remote_copy(
            src_ref=ROW.at[pl.ds(0, 1)],
            dst_ref=GATH.at[pl.ds(me, 1)],
            send_sem=lsem.at[7],
            recv_sem=lsem.at[8],
            device_id=peer,
            device_id_type=MESH,
        ).start()
    all_rows = GATH.at[pl.ds(0, len(peers))]
    pltpu.make_async_copy(all_rows, all_rows, lsem.at[8]).wait()
    totals = jnp.sum(GATH[...], axis=0, keepdims=True)
    def at(i):
        return jnp.sum(jnp.where(one_lane == i, totals, 0.0), axis=1, keepdims=True)

    b0, m00, b1, m01, m11, b2, m02, m12, m22 = [at(i) for i in range(9)]
    l10, l20 = m01 / m00, m02 / m00
    d1 = m11 - m01 * l10
    e1 = m12 - m02 * l10
    l21 = e1 / d1
    d2 = m22 - m02 * l20 - e1 * l21
    z1 = b1 - l10 * b0
    z2 = b2 - l20 * b0 - l21 * z1
    y2 = z2 / d2
    y1 = z1 / d1 - l21 * y2
    y0 = b0 / m00 - l10 * y1 - l20 * y2

    for l in range(LV):
        for t in range(2):
            NEW[l, :, 128 * t : 128 * t + 128] = (
                S[t, l, OWN_ROWS, :]
                + y0 * Q0[t, l, OWN_ROWS, :]
                + y1 * Q1[t, l, OWN_ROWS, :]
                + y2 * Q2[t, l, OWN_ROWS, :]
            )
        if l % 6 == 5:
            done = pl.ds(l - 5, 6)
            results.append(
                pltpu.make_async_copy(NEW.at[done], out.at[0, done], lsem.at[9 + len(results)])
            )
            results[-1].start()
    pltpu.make_async_copy(all_rows, all_rows, lsem.at[7]).wait()
    for copy in sends:
        copy.wait_send()
    for copy in results:
        copy.wait()


def deliver(fields, flux, fields_out, flux_out, held, held_flux, sem_in, sem_out):
    thirds = [pl.ds(i * (LV // 3), LV // 3) for i in range(3)]
    copies = [(fields.at[0, at], held.at[at], fields_out.at[0, at]) for at in thirds]
    copies.append((flux, held_flux, flux_out))
    into = [pltpu.make_async_copy(a, b, sem_in.at[i]) for i, (a, b, _) in enumerate(copies)]
    back = [pltpu.make_async_copy(b, c, sem_out.at[i]) for i, (_, b, c) in enumerate(copies)]
    for copy in into:
        copy.start()
    for arrived, copy in zip(into, back):
        arrived.wait()
        copy.start()
    for copy in back:
        copy.wait()


def body(state, conduct, storage, surface, kinds, ptab, lw, rows, rw):
    hbm = pl.BlockSpec(memory_space=pltpu.HBM)
    smem = pl.BlockSpec(memory_space=pltpu.SMEM)
    field = pltpu.VMEM((TILES, LV, EX, 128), F32)
    inner = pltpu.VMEM((2, LV, EX, 128), F32)
    plane = pltpu.VMEM((RX, CY), F32)
    pack = pltpu.VMEM((RX, 128), F32)
    landing = pltpu.VMEM((EX, 128), F32)
    shapes = (
        jax.ShapeDtypeStruct((1, LV, RX, CY), F32),
        jax.ShapeDtypeStruct((1, RX, CY), F32),
    )
    fields, flux = pl.pallas_call(
        kernel,
        out_shape=shapes,
        in_specs=[hbm, hbm, smem, hbm, hbm, smem, smem, smem, hbm],
        out_specs=(hbm, hbm),
        scratch_shapes=[
            inner,
            field,
            field,
            field,
            field,
            pltpu.VMEM((TILES, LV + 1, EX, 128), F32),
            field,
            field,
            field,
            inner,
            inner,
            pltpu.VMEM((NS, RX, CY), F32),
            plane,
            pltpu.VMEM((RX, CY), jnp.int32),
            pltpu.VMEM((CY, PATCH), F32),
            pltpu.VMEM((2 + 2 * NS, RX, CY), F32),
            plane,
            pack,
            pack,
            landing,
            landing,
            pack,
            pack,
            landing,
            landing,
            pack,
            pack,
            landing,
            landing,
            pltpu.VMEM((8, 128), F32),
            pltpu.VMEM((64, 128), F32),
            pltpu.VMEM((LV, RX, CY), F32),
            plane,
            pltpu.SemaphoreType.DMA((16,)),
            pltpu.SemaphoreType.DMA((32,)),
            pltpu.SemaphoreType.DMA((32,)),
            pltpu.SemaphoreType.REGULAR,
            pltpu.SemaphoreType.REGULAR,
        ],
        compiler_params=pltpu.CompilerParams(
            collective_id=0, has_side_effects=True, vmem_limit_bytes=66_000_000
        ),
    )(state, conduct, storage.reshape(1, 1), surface, kinds, ptab.T, jnp.transpose(lw, (2, 0, 1)), rows, rw)
    return pl.pallas_call(
        deliver,
        out_shape=shapes,
        in_specs=[hbm, hbm],
        out_specs=(hbm, hbm),
        scratch_shapes=[
            pltpu.VMEM((LV, RX, CY), F32),
            pltpu.VMEM((1, RX, CY), F32),
            pltpu.SemaphoreType.DMA((4,)),
            pltpu.SemaphoreType.DMA((4,)),
        ],
        compiler_params=pltpu.CompilerParams(vmem_limit_bytes=66_000_000),
    )(fields, flux)


def solution(mesh):
    in_specs = (
        P("comp", None, "gx", "gy"),
        P("comp", None, "gx", "gy"),
        P("comp"),
        P("comp", "gx", "gy"),
        P("comp", "gx", "gy"),
        P(),
        P(),
        P("comp", "gx"),
        P("comp", "gy", None),
    )
    out_specs = (P("comp", None, "gx", "gy"), P("comp", "gx", "gy"))
    return jax.shard_map(body, mesh=mesh, in_specs=in_specs, out_specs=out_specs, check_vma=False)
```
